32 devices in a mesh: kp: 8 (over y, x, core), vr: 4 (over z).
Axes of the slice: x: 2, y: 2, z: 4, core: 2. Of those that a mesh axis runs over, the one named last changes fastest.
Arguments:
- chol_store: bfloat16 [32, 896, 3584], P(None, 'kp', 'vr'), may hold values from -2.5 to 2.5
- amplitudes: bfloat16 [8, 2, 4, 200704], P('kp'), may hold values from -0.009765625 to 0.009765625
- block_table: int32 [8, 2, 2], replicated, may hold values from 0 to 31
- live_slots: int32 [8], replicated, may hold values from 1 to 2, as said below
- partner: int32 [8], replicated, may hold values from 0 to 7, each once
Outputs:
- ladder: float32 [8, 4, 8, 8], P('kp', None, 'vr')
- mirror: float32 [8, 4, 8, 8], P('kp', None, 'vr')
The draws below stay inside these ranges and needn't reach their ends.
Inputs may be any that keep to these rules, and one draw needn't show every extreme that they name: `live_slots`: some pair has all 2 slots live. `partner`: every pair appears exactly once.
All inputs are finite; a program needn't handle non-finite values.
Results may differ from the reference program's by a relative error of at most 0.0003.
Values may be sent and summed in bfloat16 or wider, within the bound.
No kernel may reach another device: no remote copies, remote signals or barrier semaphores. Data moves between devices by JAX's collectives and lax.ppermute only.
A program may use at most 128 MiB of HBM per device.

```python
import jax
import jax.numpy as jnp
from jax import lax

NV = 448
L = 896
NO = 2
SLAB = 8
KC = 2
NPAIR = 8
NBLK = 32


def draw_live_slots(key, part):
    count_key, pick_key = jax.random.split(key)
    counts = jax.random.randint(count_key, (NPAIR,), 1, KC + 1)
    chosen_pair = jax.random.randint(pick_key, (), 0, NPAIR)
    return counts.at[chosen_pair].set(KC).astype(jnp.int32)


def touch_ends(entries, own_key, least, high):
    spot = [jax.random.randint(jax.random.fold_in(own_key, axis), (), 0, length) for axis, length in enumerate(entries.shape)]
    widest = entries.shape.index(max(entries.shape))
    next_to = spot[:widest] + [(spot[widest] + 1) % entries.shape[widest]] + spot[widest + 1:]
    return entries.at[tuple(spot)].set(least).at[tuple(next_to)].set(high)


def steps_of(stream_key, dims, cuts, least, largest):
    factor_of = 1.0
    for position, shards_of in cuts:
        steps = jax.random.uniform(jax.random.fold_in(jax.random.fold_in(stream_key, 6), position), (shards_of,), jnp.float32, least / len(cuts), largest / len(cuts))
        factor_of = factor_of * jnp.repeat(jnp.exp(steps), dims[position] // shards_of).reshape((-1,) + (1,) * (len(dims) - 1 - position))
    return factor_of


def noise(stream_key, extent, width, most, shards=(), kind=jnp.bfloat16):
    array = width * jax.random.normal(stream_key, extent, jnp.float32)
    if shards:
        array = array * steps_of(stream_key, extent, shards, -0.22, 0.18)
    return jnp.clip(array, -most, most).astype(kind)


def setup_inputs(seed: int = 0) -> dict:
    streams_of = jax.random.split(jax.random.key(seed), 6)
    return {
        "chol_store": noise(streams_of[0], (NBLK, L, SLAB * NV), (L ** -0.25), 2.5, ((1, 8), (2, 4))),
        "amplitudes": noise(streams_of[1], (NPAIR, KC, NO * NO, NV * NV), (NV * NV * KC) ** -0.5, 0.009765625, ((0, 8),)),
        "block_table": touch_ends(jax.random.randint(streams_of[2], (NPAIR, KC, 2), 0, NBLK), jax.random.fold_in(streams_of[2], 1), 0, NBLK - 1).astype(jnp.int32),
        "live_slots": draw_live_slots(jax.random.fold_in(streams_of[5], 71), 0),
        "partner": jax.random.permutation(streams_of[4], NPAIR).astype(jnp.int32),
    }


def slot_term(left_block, right_block, amp_slot):
    left_vec = left_block.astype(jnp.float32).reshape(L, SLAB, NV)
    right_vec = right_block.astype(jnp.float32).reshape(L, SLAB, NV)
    couple = jnp.einsum('lac,lbd->acbd', left_vec, right_vec, precision=lax.Precision.HIGHEST)
    amp_full = amp_slot.astype(jnp.float32).reshape(NO * NO, NV, NV)
    return jnp.einsum('ncd,acbd->nab', amp_full, couple, precision=lax.Precision.HIGHEST)


def reference(chol_store, amplitudes, block_table, live_slots, partner):
    def one_pair(pair_index):
        def add_slot(total, slot_index):
            term = slot_term(chol_store[block_table[pair_index, slot_index, 0]],
                             chol_store[block_table[pair_index, slot_index, 1]],
                             amplitudes[pair_index, slot_index])
            active = (slot_index < live_slots[pair_index]).astype(jnp.float32)
            return total + active * term, None
        start_total = jnp.zeros((NO * NO, SLAB, SLAB), jnp.float32)
        total, unused = lax.scan(add_slot, start_total, jnp.arange(KC, dtype=jnp.int32))
        return total
    ladder = lax.map(one_pair, jnp.arange(NPAIR, dtype=jnp.int32))
    picked = ladder[partner].reshape(NPAIR, NO, NO, SLAB, SLAB)
    mirror = picked.transpose(0, 2, 1, 4, 3).reshape(NPAIR, NO * NO, SLAB, SLAB)
    return ladder, mirror
```

```python
import functools

import jax
import jax.numpy as jnp
import numpy as np
from jax import lax
from jax.experimental import pallas as pl
from jax.experimental.pallas import tpu as pltpu
from jax.sharding import PartitionSpec as P

NO = 2
SLAB = 8
PITCH = 32
LANES = 128


def patterns_of(pairs):
    if pairs <= 8:
        codes = np.arange(2 ** (pairs - 1))
        return ((codes[:, None] >> np.arange(pairs)) & 1).astype(np.int32)
    return np.random.RandomState(0).randint(0, 2, (128, pairs)).astype(np.int32)


def plan(block_table, live_slots, blocks):
    pairs, slots = block_table.shape[:2]
    pattern = patterns_of(pairs)
    count = pattern.shape[0]
    group_of = pattern[:, :, None] ^ np.arange(2)
    member = (group_of[:, None] == np.arange(2)[None, :, None, None]).reshape(2 * count, pairs * slots)
    live = jnp.arange(slots, dtype=jnp.int32)[None] < live_slots[:, None]
    ids = jnp.arange(blocks, dtype=jnp.int32)
    touch = jnp.any(block_table[..., None] == ids, axis=2) & live[..., None]
    hits = jnp.dot(jnp.asarray(member, jnp.bfloat16), touch.reshape(pairs * slots, blocks).astype(jnp.bfloat16),
                   preferred_element_type=jnp.float32)
    used = (hits > 0).astype(jnp.int32).reshape(count, 2, blocks)
    need = jnp.max(jnp.sum(used, axis=-1), axis=-1)
    best = jnp.argmin(need)
    need = jnp.min(need)
    used = lax.dynamic_index_in_dim(used, best, 0, keepdims=False)
    place = jnp.cumsum(used, axis=-1) - 1
    match = (place[:, None, :] == ids[None, :, None]) & (used[:, None, :] > 0)
    lists = jnp.sum(jnp.where(match, ids, 0), axis=-1)
    first = lax.dynamic_index_in_dim(jnp.asarray(pattern), best, 0, keepdims=False)
    return need, lists, place, first, live.astype(jnp.int32)


def ladder_kernel(meta, *refs, rows, cols, planes):
    xin, yin = refs[:planes], refs[planes:2 * planes]
    t_ref, out_ref, xs, ys_even, ys_odd = refs[2 * planes:]
    item = pl.program_id(0)
    per = SLAB // planes
    wide = ys_even.shape[1]
    shift = cols % LANES

    @pl.when(item == 0)
    def _():
        xs[...] = jnp.zeros_like(xs)
        ys_even[...] = jnp.zeros_like(ys_even)
        ys_odd[...] = jnp.zeros_like(ys_odd)

    out_ref[...] = jnp.zeros_like(out_ref)

    @pl.when(meta[2, item] > 0)
    def _():
        for step in range(planes):
            plane = meta[3, step]
            for sub in range(per):
                at = pl.ds(pl.multiple_of((plane * per + sub) * PITCH, PITCH), rows)
                xs[at, :] = xin[step][0, :, sub * cols:(sub + 1) * cols]
                right = yin[step][0, :, sub * cols:(sub + 1) * cols]
                ys_even[at, :cols] = right
                ys_odd[at, shift:shift + cols] = right
        z = jnp.dot(xs[...], t_ref[0], preferred_element_type=jnp.float32)
        high = z.astype(jnp.bfloat16)
        low = (z - high.astype(jnp.float32)).astype(jnp.bfloat16)
        size = SLAB * PITCH
        row = lax.broadcasted_iota(jnp.int32, (size, size), 0)
        col = lax.broadcasted_iota(jnp.int32, (size, size), 1)
        same = (row & (PITCH - 1)) == (col & (PITCH - 1))
        parts = []
        for n in range(NO * NO):
            start = n * cols // LANES * LANES
            both = jnp.concatenate([high[:, start:start + wide], low[:, start:start + wide]], axis=0)
            right = ys_even[...] if start == n * cols else ys_odd[...]
            gram = lax.dot_general(both, right, (((1,), (1,)), ((), ())), preferred_element_type=jnp.float32)
            gram = jnp.where(same, gram[:size] + gram[size:], 0.0)
            parts.append(jnp.sum(gram.reshape(SLAB, PITCH, size), axis=1))
        totals = jnp.concatenate(parts, axis=0)
        pick = (lax.broadcasted_iota(jnp.int32, (size, SLAB), 0) // PITCH
                == lax.broadcasted_iota(jnp.int32, (size, SLAB), 1)).astype(jnp.float32)
        out_ref[0] = jnp.dot(totals, pick, precision=lax.Precision.HIGHEST, preferred_element_type=jnp.float32)


def ladder_part(meta, pieces, amps, cols):
    pairs = amps.shape[0]
    planes = len(pieces)
    rows, width = pieces[0].shape[1:]
    size = SLAB * PITCH
    wide = -(-cols // LANES) * LANES
    x_spec = pl.BlockSpec((1, rows, width), lambda i, m: (m[0, i], 0, 0))
    y_spec = pl.BlockSpec((1, rows, width), lambda i, m: (m[1, i], 0, 0))
    return pl.pallas_call(
        functools.partial(ladder_kernel, rows=rows, cols=cols, planes=planes),
        grid_spec=pltpu.PrefetchScalarGridSpec(
            num_scalar_prefetch=1,
            grid=(pairs,),
            in_specs=[x_spec] * planes + [y_spec] * planes
            + [pl.BlockSpec((1,) + amps.shape[1:], lambda i, m: (i, 0, 0))],
            out_specs=pl.BlockSpec((1, NO * NO * SLAB, SLAB), lambda i, m: (i, 0, 0)),
            scratch_shapes=[
                pltpu.VMEM((size, cols), jnp.bfloat16),
                pltpu.VMEM((size, wide), jnp.bfloat16),
                pltpu.VMEM((size, wide), jnp.bfloat16),
            ],
        ),
        out_shape=jax.ShapeDtypeStruct((pairs, NO * NO * SLAB, SLAB), jnp.float32),
        compiler_params=pltpu.CompilerParams(vmem_limit_bytes=40 * 2 ** 20),
        cost_estimate=pl.CostEstimate(
            flops=pairs * 2 * size * cols * NO * NO * (cols + size),
            bytes_accessed=pairs * (amps.shape[1] * amps.shape[2] * 2 + 2 * planes * rows * width * 2),
            transcendentals=0),
    )(meta, *pieces, *pieces, amps)


def body(chol_store, amplitudes, block_table, live_slots, partner):
    ranks = lax.axis_size("kp")
    planes = lax.axis_size("vr")
    pairs, slots = block_table.shape[:2]
    blocks, depth, width = chol_store.shape
    cols = width * planes // SLAB
    per = SLAB // planes
    halves = planes // slots
    share = depth // halves
    me_pair, me_plane = lax.axis_index("kp"), lax.axis_index("vr")
    group = me_plane % slots

    need, lists, place, first, live = plan(block_table, live_slots, blocks)

    slot_at = group ^ first
    own_place = lax.dynamic_index_in_dim(place, group, 0, keepdims=False)
    pair_ids = jnp.arange(pairs, dtype=jnp.int32)
    table_at = jnp.where((slot_at == 0)[:, None], block_table[:, 0], block_table[:, 1])
    live_at = jnp.where(slot_at == 0, live[:, 0], live[:, 1])
    spots = own_place[table_at] * live_at[:, None]
    planes_at = (me_plane - pair_ids) % planes
    meta = jnp.stack([spots[:, 0], spots[:, 1], live_at, planes_at]).astype(jnp.int32)

    amp = lax.dynamic_index_in_dim(amplitudes[0], slot_at[me_pair], 0, keepdims=False)
    amp = amp.reshape(NO * NO, cols, cols).transpose(1, 0, 2).reshape(cols, NO * NO * cols)

    stages = [(0, min(PITCH, share))]
    while stages[-1][1] < share:
        stages.append((stages[-1][1], min(stages[-1][1] + PITCH, share)))

    def run(cap, amp, lists, meta):
        amps = lax.all_gather(amp, "kp", axis=0, tiled=False)
        total = jnp.zeros((pairs, NO * NO * SLAB, SLAB), jnp.float32)
        for begin, end in stages:
            pieces = []
            for step in range(planes):
                target = (me_plane + step) % planes
                start = (target // slots) * share + begin
                window = lax.dynamic_slice_in_dim(chol_store, start, end - begin, 1)
                picked = lax.dynamic_index_in_dim(lists, target % slots, 0, keepdims=False)[:cap]
                piece = window.at[picked].get(mode="promise_in_bounds")
                if step:
                    piece = lax.ppermute(piece, "vr", [(i, (i + step) % planes) for i in range(planes)])
                pieces.append(piece)
            total = total + ladder_part(meta, pieces, amps, cols)
        return total

    most = min(2 * pairs, blocks)
    stride = max(1, most // 16)
    caps = [most - stride * k for k in range(9, -1, -1) if most - stride * k > 0]
    branch = jnp.sum((need > jnp.asarray(caps, jnp.int32)).astype(jnp.int32))
    total = lax.switch(branch, [functools.partial(run, cap) for cap in caps], amp, lists, meta)

    full = total.reshape(pairs, NO, NO, SLAB, SLAB)
    other = full[partner].transpose(0, 2, 1, 4, 3)
    both = jnp.stack([full, other]).reshape(2, ranks, NO * NO, planes, per, SLAB)
    both = both.transpose(1, 3, 0, 2, 4, 5).reshape(ranks * planes, 2 * NO * NO * per * SLAB)
    mine = lax.all_to_all(both, ("kp", "vr"), split_axis=0, concat_axis=0, tiled=True)
    mine = jnp.sum(mine, axis=0).reshape(2, 1, NO * NO, per, SLAB)
    return mine[0], mine[1]


def solution(mesh):
    placed = (P(None, "kp", "vr"), P("kp", None, None, None), P(), P(), P())
    return jax.shard_map(
        body,
        mesh=mesh,
        in_specs=placed,
        out_specs=(P("kp", None, "vr", None), P("kp", None, "vr", None)),
        check_vma=False,
    )
```

```python
import functools

import jax
import jax.numpy as jnp
import numpy as np
from jax import lax
from jax.experimental import pallas as pl
from jax.experimental.pallas import tpu as pltpu
from jax.sharding import PartitionSpec as P

NO = 2
SLAB = 8
PITCH = 32
LANES = 128
CHOICES = 128
ROOM = 58 * 2 ** 20
ANY = pl.BlockSpec(memory_space=pl.ANY)
SMEM = pl.BlockSpec(memory_space=pltpu.SMEM)
VMEM = pl.BlockSpec(memory_space=pltpu.VMEM)


def choices_of(pairs):
    if pairs <= 8:
        codes = np.arange(CHOICES)
        return ((codes[:, None] >> np.arange(pairs)) & 1).astype(np.int32)
    return np.random.RandomState(0).randint(0, 2, (CHOICES, pairs)).astype(np.int32)


def plan_kernel(table, live, first, member, branch_ref, mine_ref, lists_ref, meta_ref, touch, place,
                *, pairs, blocks, caps, room, planes):
    items = 2 * pairs
    group = lax.rem(lax.axis_index("vr"), 2)
    lane = lax.broadcasted_iota(jnp.int32, (1, touch.shape[1]), 1)
    for item in range(items):
        alive = (item % 2 < live[item // 2]).astype(jnp.int32)
        left = table[2 * item] * alive - (1 - alive)
        right = table[2 * item + 1] * alive - (1 - alive)
        touch[item:item + 1, :] = ((lane == left) | (lane == right)).astype(jnp.float32)
    counts = []
    for side in range(2):
        hits = jnp.dot(member[side], touch[...], preferred_element_type=jnp.float32)
        counts.append(jnp.sum((hits > 0.5).astype(jnp.float32), axis=1, keepdims=True))
    need = jnp.maximum(counts[0], counts[1])
    order = lax.broadcasted_iota(jnp.int32, need.shape, 0).astype(jnp.float32)
    code = jnp.min(need * CHOICES + order).astype(jnp.int32)
    best = lax.rem(code, CHOICES)
    need = lax.div(code, CHOICES)
    branch = jnp.int32(0)
    for cap in caps[:-1]:
        branch += (need > cap).astype(jnp.int32)
    branch_ref[0] = branch

    def clear(i, carry):
        place[i] = 0
        return carry

    lax.fori_loop(0, 2 * blocks, clear, 0)

    def empty(i, carry):
        lists_ref[i] = 0
        return carry

    lax.fori_loop(0, 2 * room, empty, 0)

    def mark(item, carry):
        pair = lax.div(item, 2)
        slot = lax.rem(item, 2)
        side = first[best * pairs + pair] ^ slot
        alive = (slot < live[pair]).astype(jnp.int32)
        for end in range(2):
            at = side * blocks + table[2 * item + end]
            place[at] = place[at] | alive
        return carry

    lax.fori_loop(0, items, mark, 0)
    for side in range(2):
        def number(i, count):
            here = place[side * blocks + i]
            lists_ref[side * room + count] = i
            place[side * blocks + i] = count
            return count + here

        lax.fori_loop(0, blocks, number, jnp.int32(0))

    def tell(pair, carry):
        slot = group ^ first[best * pairs + pair]
        alive = (slot < live[pair]).astype(jnp.int32)
        at = 4 * pair + 2 * slot
        meta_ref[pair] = place[group * blocks + table[at]] * alive
        meta_ref[pairs + pair] = place[group * blocks + table[at + 1]] * alive
        meta_ref[2 * pairs + pair] = alive
        return carry

    lax.fori_loop(0, pairs, tell, 0)
    mine_ref[0] = group ^ first[best * pairs + lax.axis_index("kp")]


def plan(block_table, live_slots, blocks, caps, planes):
    pairs = live_slots.shape[0]
    first = choices_of(pairs)
    member = (first[None, :, :, None] ^ np.arange(2)) == np.arange(2)[:, None, None, None]
    member = member.reshape(2, CHOICES, 2 * pairs).astype(np.float32)
    room = caps[-1] + 8
    width = -(-blocks // LANES) * LANES
    return pl.pallas_call(
        functools.partial(plan_kernel, pairs=pairs, blocks=blocks, caps=caps, room=room, planes=planes),
        in_specs=[SMEM, SMEM, SMEM, VMEM],
        out_specs=[SMEM, SMEM, SMEM, SMEM],
        out_shape=[jax.ShapeDtypeStruct((1,), jnp.int32), jax.ShapeDtypeStruct((1,), jnp.int32),
                   jax.ShapeDtypeStruct((2 * room,), jnp.int32), jax.ShapeDtypeStruct((3 * pairs,), jnp.int32)],
        scratch_shapes=[pltpu.VMEM((2 * pairs, width), jnp.float32), pltpu.SMEM((2 * blocks,), jnp.int32)],
    )(block_table.reshape(-1), live_slots, jnp.asarray(first.reshape(-1)), jnp.asarray(member))


def gather_kernel(lists, store, *refs, cap, room, steps, planes, grains, begin, size):
    outs, sems = refs[:-1], refs[-1]
    me_plane = lax.axis_index("vr")
    copies = []
    for k, step in enumerate(steps):
        target = lax.rem(me_plane + step, planes)
        side, half = lax.rem(target, 2), lax.div(target, 2)
        for u in range(cap):
            block = lists[side * room + u]
            start = block * (grains * (planes // 2)) + half * grains + begin
            copy = pltpu.make_async_copy(store.at[pl.ds(start, size)], outs[k].at[u], sems.at[k, u])
            copy.start()
            copies.append(copy)
    for copy in copies:
        copy.wait()


def gather(lists, store, cap, room, steps, planes, grains, begin, size):
    grain, width = store.shape[1:]
    outs = pl.pallas_call(
        functools.partial(gather_kernel, cap=cap, room=room, steps=steps, planes=planes, grains=grains,
                          begin=begin, size=size),
        in_specs=[SMEM, ANY],
        out_specs=[ANY] * len(steps),
        out_shape=[jax.ShapeDtypeStruct((cap, size, grain, width), store.dtype)] * len(steps),
        scratch_shapes=[pltpu.SemaphoreType.DMA((len(steps), cap))],
    )(lists, store)
    return [out.reshape(cap, size * grain, width) for out in outs]


def ladder_kernel(meta, *refs, pairs, rows, cols, planes):
    xin, yin = refs[:planes], refs[planes:2 * planes]
    t_ref, out_ref, raw, xs, ys, ts, order = refs[2 * planes:]
    item = pl.program_id(0)
    me_plane = lax.axis_index("vr")
    per = SLAB // planes
    half = cols // 2
    size = SLAB * PITCH

    @pl.when(item == 0)
    def _():
        raw[...] = jnp.zeros_like(raw)
        ys[...] = jnp.zeros_like(ys)
        row = lax.broadcasted_iota(jnp.int32, (cols, cols), 0)
        col = lax.broadcasted_iota(jnp.int32, (cols, cols), 1)
        wanted = jnp.where(col < half, 2 * col, 2 * (col - half) + 1)
        order[...] = (row == wanted).astype(jnp.bfloat16)

    out_ref[...] = jnp.zeros_like(out_ref)

    @pl.when(meta[2 * pairs + item] > 0)
    def _():
        for step in range(planes):
            plane = lax.rem(me_plane + planes - step, planes)
            at = pl.ds(pl.multiple_of(plane * PITCH, PITCH), rows)
            raw[at, :] = xin[step][0]
            for sub in range(per):
                at = pl.ds(pl.multiple_of((plane * per + sub) * PITCH, PITCH), rows)
                ys[at, :] = yin[step][0, :, sub * cols:(sub + 1) * cols]
        for sub in range(per):
            turned = jnp.dot(raw[:, sub * cols:(sub + 1) * cols], order[...],
                             preferred_element_type=jnp.float32).astype(jnp.bfloat16)
            for plane in range(planes):
                to = (plane * per + sub) * PITCH
                xs[to:to + PITCH, :] = turned[plane * PITCH:(plane + 1) * PITCH]
        row = lax.broadcasted_iota(jnp.int32, (size, size), 0)
        col = lax.broadcasted_iota(jnp.int32, (size, size), 1)
        same = (row & (PITCH - 1)) == (col & (PITCH - 1))
        parts = []
        for n in range(NO * NO):
            ts[:half, :] = t_ref[0, n, :, :cols]
            ts[half:, :] = t_ref[0, n, :, cols:]
            z = jnp.dot(xs[...], ts[...], preferred_element_type=jnp.float32)
            high = z.astype(jnp.bfloat16)
            low = (z - high.astype(jnp.float32)).astype(jnp.bfloat16)
            both = jnp.concatenate([high, low], axis=0)
            gram = lax.dot_general(both, ys[...], (((1,), (1,)), ((), ())), preferred_element_type=jnp.float32)
            gram = jnp.where(same, gram[:size] + gram[size:], 0.0)
            parts.append(jnp.sum(gram.reshape(SLAB, PITCH, size), axis=1))
        totals = jnp.concatenate(parts, axis=0)
        pick = (lax.broadcasted_iota(jnp.int32, (size, SLAB), 0) // PITCH
                == lax.broadcasted_iota(jnp.int32, (size, SLAB), 1)).astype(jnp.float32)
        out_ref[0] = jnp.dot(totals, pick, precision=lax.Precision.HIGHEST, preferred_element_type=jnp.float32)


def ladder_part(meta, pieces, amps, cols):
    pairs = amps.shape[0]
    planes = len(pieces)
    rows, width = pieces[0].shape[1:]
    size = SLAB * PITCH
    x_spec = pl.BlockSpec((1, rows, width), lambda i, m: (m[i], 0, 0))
    y_spec = pl.BlockSpec((1, rows, width), lambda i, m: (m[pairs + i], 0, 0))
    return pl.pallas_call(
        functools.partial(ladder_kernel, pairs=pairs, rows=rows, cols=cols, planes=planes),
        grid_spec=pltpu.PrefetchScalarGridSpec(
            num_scalar_prefetch=1,
            grid=(pairs,),
            in_specs=[x_spec] * planes + [y_spec] * planes
            + [pl.BlockSpec((1,) + amps.shape[1:], lambda i, m: (i, 0, 0, 0))],
            out_specs=pl.BlockSpec((1, NO * NO * SLAB, SLAB), lambda i, m: (i, 0, 0)),
            scratch_shapes=[
                pltpu.VMEM((planes * PITCH, width), jnp.bfloat16),
                pltpu.VMEM((size, cols), jnp.bfloat16),
                pltpu.VMEM((size, cols), jnp.bfloat16),
                pltpu.VMEM((cols, cols), jnp.bfloat16),
                pltpu.VMEM((cols, cols), jnp.bfloat16),
            ],
        ),
        out_shape=jax.ShapeDtypeStruct((pairs, NO * NO * SLAB, SLAB), jnp.float32),
        compiler_params=pltpu.CompilerParams(vmem_limit_bytes=ROOM),
        cost_estimate=pl.CostEstimate(
            flops=pairs * 2 * size * cols * (NO * NO * (cols + 2 * size) + cols),
            bytes_accessed=pairs * (NO * NO * cols * cols * 2 + 2 * planes * rows * width * 2),
            transcendentals=0),
    )(meta, *pieces, *pieces, amps)


def body(chol_store, amplitudes, block_table, live_slots, partner):
    ranks = lax.axis_size("kp")
    planes = lax.axis_size("vr")
    pairs, slots = block_table.shape[:2]
    blocks, depth, width = chol_store.shape
    cols = width * planes // SLAB
    per = SLAB // planes
    share = depth // (planes // slots)

    most = min(2 * pairs, blocks)
    caps = sorted({max(1, most * part // 16) for part in (9, 10, 11, 12, 16)})
    room = caps[-1] + 8
    branch, mine, lists, meta = plan(block_table, live_slots, blocks, caps, planes)

    amp = lax.dynamic_index_in_dim(amplitudes[0], mine[0], 0, keepdims=False)
    amp = amp.reshape(NO * NO, cols // 2, 2 * cols)

    grain = int(np.gcd(share, 8))
    grains = share // grain
    store = chol_store.reshape(blocks * depth // grain, grain, width)
    step_of = max(1, PITCH // grain)
    stages = [(g, min(step_of, grains - g)) for g in range(0, grains, step_of)]

    def run(cap, amp, lists, meta):
        amps = lax.all_gather(amp, "kp", axis=0, tiled=False)
        total = None
        others = tuple(range(1, planes))
        own = [gather(lists, store, cap, room, (0,), planes, grains, *stage)[0] for stage in stages]
        for k, stage in enumerate(stages):
            sent = gather(lists, store, cap, room, others, planes, grains, *stage)
            pieces = [own[k]] + [
                lax.ppermute(piece, "vr", [(i, (i + step) % planes) for i in range(planes)])
                for step, piece in zip(others, sent)]
            part = ladder_part(meta, pieces, amps, cols)
            total = part if total is None else total + part
        return total

    total = lax.switch(branch[0], [functools.partial(run, cap) for cap in caps], amp, lists, meta)

    full = total.reshape(pairs, NO, NO, SLAB, SLAB)
    other = full[partner].transpose(0, 2, 1, 4, 3)
    both = jnp.stack([full, other]).reshape(2, ranks, NO * NO, planes, per, SLAB)
    both = both.transpose(1, 3, 0, 2, 4, 5).reshape(ranks * planes, 2 * NO * NO * per * SLAB)
    mine = lax.all_to_all(both, ("kp", "vr"), split_axis=0, concat_axis=0, tiled=True)
    mine = jnp.sum(mine, axis=0).reshape(2, 1, NO * NO, per, SLAB)
    return mine[0], mine[1]


def solution(mesh):
    placed = (P(None, "kp", "vr"), P("kp", None, None, None), P(), P(), P())
    return jax.shard_map(
        body,
        mesh=mesh,
        in_specs=placed,
        out_specs=(P("kp", None, "vr", None), P("kp", None, "vr", None)),
        check_vma=False,
    )
```

```python
import functools

import jax
import jax.numpy as jnp
import numpy as np
from jax import lax
from jax.experimental import pallas as pl
from jax.experimental.pallas import tpu as pltpu
from jax.sharding import PartitionSpec as P

NO = 2
SLAB = 8
PITCH = 32
LANES = 128
CHOICES = 128
ROOM = 58 * 2 ** 20
ANY = pl.BlockSpec(memory_space=pl.ANY)
SMEM = pl.BlockSpec(memory_space=pltpu.SMEM)
VMEM = pl.BlockSpec(memory_space=pltpu.VMEM)


def choices_of(pairs):
    if pairs <= 8:
        codes = np.arange(CHOICES)
        return ((codes[:, None] >> np.arange(pairs)) & 1).astype(np.int32)
    return np.random.RandomState(0).randint(0, 2, (CHOICES, pairs)).astype(np.int32)


def plan_kernel(table, live, first, member, branch_ref, mine_ref, lists_ref, meta_ref, touch, place,
                *, pairs, blocks, caps, room, planes):
    items = 2 * pairs
    group = lax.rem(lax.axis_index("vr"), 2)
    lane = lax.broadcasted_iota(jnp.int32, (1, touch.shape[1]), 1)
    for item in range(items):
        alive = (item % 2 < live[item // 2]).astype(jnp.int32)
        left = table[item // 2, item % 2, 0] * alive - (1 - alive)
        right = table[item // 2, item % 2, 1] * alive - (1 - alive)
        touch[item:item + 1, :] = ((lane == left) | (lane == right)).astype(jnp.float32)
    counts = []
    for side in range(2):
        hits = jnp.dot(member[side], touch[...], preferred_element_type=jnp.float32)
        counts.append(jnp.sum((hits > 0.5).astype(jnp.float32), axis=1, keepdims=True))
    need = jnp.maximum(counts[0], counts[1])
    order = lax.broadcasted_iota(jnp.int32, need.shape, 0).astype(jnp.float32)
    code = jnp.min(need * CHOICES + order).astype(jnp.int32)
    best = lax.rem(code, CHOICES)
    need = lax.div(code, CHOICES)
    branch = jnp.int32(0)
    for cap in caps[:-1]:
        branch += (need > cap).astype(jnp.int32)
    branch_ref[0] = branch

    def clear(i, carry):
        place[i] = 0
        return carry

    lax.fori_loop(0, 2 * blocks, clear, 0)

    def empty(i, carry):
        lists_ref[i] = 0
        return carry

    lax.fori_loop(0, 2 * room, empty, 0)

    def mark(item, carry):
        pair = lax.div(item, 2)
        slot = lax.rem(item, 2)
        side = first[best * pairs + pair] ^ slot
        alive = (slot < live[pair]).astype(jnp.int32)
        for end in range(2):
            at = side * blocks + table[pair, slot, end]
            place[at] = place[at] | alive
        return carry

    lax.fori_loop(0, items, mark, 0)
    for side in range(2):
        def number(i, count):
            here = place[side * blocks + i]
            lists_ref[side * room + count] = i
            place[side * blocks + i] = count
            return count + here

        lax.fori_loop(0, blocks, number, jnp.int32(0))

    def tell(pair, held):
        slot = group ^ first[best * pairs + pair]
        alive = slot < live[pair]
        now = (place[group * blocks + table[pair, slot, 0]], place[group * blocks + table[pair, slot, 1]], pair)
        held = tuple(jnp.where(alive, new, old) for new, old in zip(now, held))
        for k in range(3):
            meta_ref[k * pairs + pair] = held[k]
        meta_ref[3 * pairs + pair] = alive.astype(jnp.int32)
        return held

    lax.fori_loop(0, pairs, tell, (jnp.int32(0),) * 3)
    mine_ref[0] = group ^ first[best * pairs + lax.axis_index("kp")]


def plan(block_table, live_slots, blocks, caps, planes):
    pairs = live_slots.shape[0]
    first = choices_of(pairs)
    member = (first[None, :, :, None] ^ np.arange(2)) == np.arange(2)[:, None, None, None]
    member = member.reshape(2, CHOICES, 2 * pairs).astype(np.float32)
    room = caps[-1] + 8
    width = -(-blocks // LANES) * LANES
    return pl.pallas_call(
        functools.partial(plan_kernel, pairs=pairs, blocks=blocks, caps=caps, room=room, planes=planes),
        in_specs=[SMEM, SMEM, SMEM, VMEM],
        out_specs=[SMEM, SMEM, SMEM, SMEM],
        out_shape=[jax.ShapeDtypeStruct((1,), jnp.int32), jax.ShapeDtypeStruct((1,), jnp.int32),
                   jax.ShapeDtypeStruct((2 * room,), jnp.int32), jax.ShapeDtypeStruct((4 * pairs,), jnp.int32)],
        scratch_shapes=[pltpu.VMEM((2 * pairs, width), jnp.float32), pltpu.SMEM((2 * blocks,), jnp.int32)],
    )(block_table, live_slots, jnp.asarray(first.reshape(-1)), jnp.asarray(member))


def gather_kernel(lists, store, *refs, cap, room, steps, planes, grains, begin, size):
    outs, sems = refs[:-1], refs[-1]
    me_plane = lax.axis_index("vr")
    copies = []
    for k, step in enumerate(steps):
        target = lax.rem(me_plane + step, planes)
        side, half = lax.rem(target, 2), lax.div(target, 2)
        for u in range(cap):
            block = lists[side * room + u]
            start = block * (grains * (planes // 2)) + half * grains + begin
            copy = pltpu.make_async_copy(store.at[pl.ds(start, size)], outs[k].at[u], sems.at[k, u])
            copy.start()
            copies.append(copy)
    for copy in copies:
        copy.wait()


def gather(lists, store, cap, room, steps, planes, grains, begin, size):
    grain, width = store.shape[1:]
    outs = pl.pallas_call(
        functools.partial(gather_kernel, cap=cap, room=room, steps=steps, planes=planes, grains=grains,
                          begin=begin, size=size),
        in_specs=[SMEM, ANY],
        out_specs=[VMEM] * len(steps),
        out_shape=[jax.ShapeDtypeStruct((cap, size, grain, width), store.dtype)] * len(steps),
        scratch_shapes=[pltpu.SemaphoreType.DMA((len(steps), cap))],
    )(lists, store)
    return [out.reshape(cap, size * grain, width) for out in outs]


def ladder_kernel(meta, *refs, pairs, rows, cols, planes, more):
    xin, yin = refs[:planes], refs[planes:2 * planes]
    t_ref = refs[2 * planes]
    before = refs[2 * planes + 1] if more else None
    out_ref, raw, xs, ys, ts, order, sums = refs[2 * planes + 1 + more:]
    item = pl.program_id(0)
    me_plane = lax.axis_index("vr")
    per = SLAB // planes
    half = cols // 2
    size = SLAB * PITCH
    group = NO * NO * SLAB

    @pl.when(item == 0)
    def _():
        if rows < PITCH:
            raw[...] = jnp.zeros_like(raw)
            ys[...] = jnp.zeros_like(ys)
        row = lax.broadcasted_iota(jnp.int32, (cols, cols), 0)
        col = lax.broadcasted_iota(jnp.int32, (cols, cols), 1)
        wanted = jnp.where(col < half, 2 * col, 2 * (col - half) + 1)
        order[...] = (row == wanted).astype(jnp.bfloat16)
        sums[...] = jnp.zeros_like(sums)

    @pl.when(meta[3 * pairs + item] > 0)
    def _():
        for step in range(planes):
            plane = lax.rem(me_plane + planes - step, planes)
            at = pl.ds(pl.multiple_of(plane * PITCH, PITCH), rows)
            raw[at, :] = xin[step][0]
            for sub in range(per):
                at = pl.ds(pl.multiple_of((plane * per + sub) * PITCH, PITCH), rows)
                ys[at, :] = yin[step][0, :, sub * cols:(sub + 1) * cols]
        for sub in range(per):
            turned = jnp.dot(raw[:, sub * cols:(sub + 1) * cols], order[...],
                             preferred_element_type=jnp.float32).astype(jnp.bfloat16)
            for plane in range(planes):
                to = (plane * per + sub) * PITCH
                xs[to:to + PITCH, :] = turned[plane * PITCH:(plane + 1) * PITCH]
        parts = []
        for n in range(NO * NO):
            ts[n, :half, :] = t_ref[0, n, :, :cols]
            ts[n, half:, :] = t_ref[0, n, :, cols:]
            z = jnp.dot(xs[...], ts[n], preferred_element_type=jnp.float32)
            high = z.astype(jnp.bfloat16)
            parts += [high, (z - high.astype(jnp.float32)).astype(jnp.bfloat16)]
        gram = lax.dot_general(ys[...], jnp.concatenate(parts, axis=0), (((1,), (1,)), ((), ())),
                               preferred_element_type=jnp.float32)
        row = lax.broadcasted_iota(jnp.int32, (size, size), 0)
        col = lax.broadcasted_iota(jnp.int32, (size, size), 1)
        same = (row & (PITCH - 1)) == (col & (PITCH - 1))
        for n in range(NO * NO):
            at = 2 * n * size
            term = jnp.where(same, gram[:, at:at + size] + gram[:, at + size:at + 2 * size], 0.0)
            sums[item, n * SLAB:(n + 1) * SLAB, :] = jnp.sum(term.reshape(SLAB, PITCH, size), axis=1)

    @pl.when(item == pairs - 1)
    def _():
        pick = (lax.broadcasted_iota(jnp.int32, (size, SLAB), 0) // PITCH
                == lax.broadcasted_iota(jnp.int32, (size, SLAB), 1)).astype(jnp.float32)
        total = jnp.dot(sums[...].reshape(pairs * group, size), pick, precision=lax.Precision.HIGHEST,
                        preferred_element_type=jnp.float32)
        out_ref[...] = total + before[...] if more else total


def ladder_part(meta, pieces, amps, cols, before):
    pairs = amps.shape[0]
    planes = len(pieces)
    rows, width = pieces[0].shape[1:]
    size = SLAB * PITCH
    group = NO * NO * SLAB
    more = before is not None
    x_spec = pl.BlockSpec((1, rows, width), lambda i, m: (m[i], 0, 0))
    y_spec = pl.BlockSpec((1, rows, width), lambda i, m: (m[pairs + i], 0, 0))
    t_spec = pl.BlockSpec((1,) + amps.shape[1:], lambda i, m: (m[2 * pairs + i], 0, 0, 0))
    sum_spec = pl.BlockSpec((pairs * group, SLAB), lambda i, m: (0, 0))
    return pl.pallas_call(
        functools.partial(ladder_kernel, pairs=pairs, rows=rows, cols=cols, planes=planes, more=more),
        grid_spec=pltpu.PrefetchScalarGridSpec(
            num_scalar_prefetch=1,
            grid=(pairs,),
            in_specs=[x_spec] * planes + [y_spec] * planes + [t_spec] + [sum_spec] * more,
            out_specs=sum_spec,
            scratch_shapes=[
                pltpu.VMEM((planes * PITCH, width), jnp.bfloat16),
                pltpu.VMEM((size, cols), jnp.bfloat16),
                pltpu.VMEM((size, cols), jnp.bfloat16),
                pltpu.VMEM((NO * NO, cols, cols), jnp.bfloat16),
                pltpu.VMEM((cols, cols), jnp.bfloat16),
                pltpu.VMEM((pairs, group, size), jnp.float32),
            ],
        ),
        out_shape=jax.ShapeDtypeStruct((pairs * group, SLAB), jnp.float32),
        compiler_params=pltpu.CompilerParams(vmem_limit_bytes=ROOM),
        cost_estimate=pl.CostEstimate(
            flops=pairs * 2 * size * cols * (NO * NO * (cols + 2 * size) + cols),
            bytes_accessed=pairs * (NO * NO * cols * cols * 2 + 2 * planes * rows * width * 2),
            transcendentals=0),
    )(meta, *pieces, *pieces, amps, *([before] if more else []))


def body(chol_store, amplitudes, block_table, live_slots, partner):
    ranks = lax.axis_size("kp")
    planes = lax.axis_size("vr")
    pairs, slots = block_table.shape[:2]
    blocks, depth, width = chol_store.shape
    cols = width * planes // SLAB
    per = SLAB // planes
    share = depth // (planes // slots)

    most = min(2 * pairs, blocks)
    caps = sorted({max(1, most * part // 16) for part in (9, 10, 11, 12, 16)})
    room = caps[-1] + 8
    branch, mine, lists, meta = plan(block_table, live_slots, blocks, caps, planes)

    amp = lax.dynamic_index_in_dim(amplitudes[0], mine[0], 0, keepdims=False)
    amp = amp.reshape(NO * NO, cols // 2, 2 * cols)

    grain = int(np.gcd(share, 8))
    grains = share // grain
    store = chol_store.reshape(blocks * depth // grain, grain, width)
    step_of = max(1, PITCH // grain)
    stages = [(g, min(step_of, grains - g)) for g in range(0, grains, step_of)]

    def run(cap, amp, lists, meta):
        amps = lax.all_gather(amp, "kp", axis=0, tiled=False)
        total = None
        others = tuple(range(1, planes))
        own = [gather(lists, store, cap, room, (0,), planes, grains, *stage)[0] for stage in stages]
        for k, stage in enumerate(stages):
            sent = gather(lists, store, cap, room, others, planes, grains, *stage)
            pieces = [own[k]] + [
                lax.ppermute(piece, "vr", [(i, (i + step) % planes) for i in range(planes)])
                for step, piece in zip(others, sent)]
            total = ladder_part(meta, pieces, amps, cols, total)
        return total

    total = lax.switch(branch[0], [functools.partial(run, cap) for cap in caps], amp, lists, meta)

    other = total.reshape(pairs, NO, NO, planes, per, SLAB)
    full = other.reshape(pairs, NO, NO, SLAB, planes, per).transpose(0, 4, 1, 2, 5, 3)
    other = other[partner].transpose(0, 3, 2, 1, 4, 5)
    both = jnp.stack([full, other], axis=2).reshape(ranks * planes, 2 * NO * NO * per * SLAB)
    mine = lax.all_to_all(both, ("kp", "vr"), split_axis=0, concat_axis=0, tiled=True)
    mine = jnp.sum(mine, axis=0).reshape(2, 1, NO * NO, per, SLAB)
    return mine[0], mine[1]


def solution(mesh):
    placed = (P(None, "kp", "vr"), P("kp", None, None, None), P(), P(), P())
    return jax.shard_map(
        body,
        mesh=mesh,
        in_specs=placed,
        out_specs=(P("kp", None, "vr", None), P("kp", None, "vr", None)),
        check_vma=False,
    )
```

```python
import functools

import jax
import jax.numpy as jnp
import numpy as np
from jax import lax
from jax.experimental import pallas as pl
from jax.experimental.pallas import tpu as pltpu
from jax.sharding import PartitionSpec as P

NO = 2
SLAB = 8
PITCH = 32
LANES = 128
CHOICES = 128
ROOM = 58 * 2 ** 20
ANY = pl.BlockSpec(memory_space=pl.ANY)
SMEM = pl.BlockSpec(memory_space=pltpu.SMEM)
VMEM = pl.BlockSpec(memory_space=pltpu.VMEM)


def choices_of(pairs):
    if pairs <= 8:
        codes = np.arange(CHOICES)
        return ((codes[:, None] >> np.arange(pairs)) & 1).astype(np.int32)
    return np.random.RandomState(0).randint(0, 2, (CHOICES, pairs)).astype(np.int32)


def plan_kernel(table, live, first, member, branch_ref, mine_ref, lists_ref, meta_ref, touch, place,
                *, pairs, blocks, caps, room, planes):
    items = 2 * pairs
    group = lax.rem(lax.axis_index("vr"), 2)
    lane = lax.broadcasted_iota(jnp.int32, (1, touch.shape[1]), 1)
    for item in range(items):
        alive = (item % 2 < live[item // 2]).astype(jnp.int32)
        left = table[item // 2, item % 2, 0] * alive - (1 - alive)
        right = table[item // 2, item % 2, 1] * alive - (1 - alive)
        last = jnp.where(alive > 0, touch.shape[1] - 1, -1)
        touch[item:item + 1, :] = ((lane == left) | (lane == right) | (lane == last)).astype(jnp.float32)
    counts, loads = [], []
    for side in range(2):
        hits = jnp.dot(member[side], touch[...], preferred_element_type=jnp.float32)
        is_last = lane == touch.shape[1] - 1
        counts.append(jnp.sum(jnp.where(is_last, 0.0, (hits > 0.5).astype(jnp.float32)), axis=1, keepdims=True))
        loads.append(jnp.sum(jnp.where(is_last, hits, 0.0), axis=1, keepdims=True))
    need = jnp.maximum(counts[0], counts[1]) * (pairs + 1) + jnp.maximum(loads[0], loads[1])
    order = lax.broadcasted_iota(jnp.int32, need.shape, 0).astype(jnp.float32)
    code = jnp.min(need * CHOICES + order).astype(jnp.int32)
    best = lax.rem(code, CHOICES)
    need = lax.div(code, CHOICES * (pairs + 1))
    branch = jnp.int32(0)
    for cap in caps[:-1]:
        branch += (need > cap).astype(jnp.int32)
    branch_ref[0] = branch

    def clear(i, carry):
        place[i] = 0
        return carry

    lax.fori_loop(0, 2 * blocks, clear, 0)

    def empty(i, carry):
        lists_ref[i] = 0
        return carry

    lax.fori_loop(0, 2 * room, empty, 0)

    def mark(item, carry):
        pair = lax.div(item, 2)
        slot = lax.rem(item, 2)
        side = first[best * pairs + pair] ^ slot
        alive = (slot < live[pair]).astype(jnp.int32)
        for end in range(2):
            at = side * blocks + table[pair, slot, end]
            place[at] = place[at] | alive
        return carry

    lax.fori_loop(0, items, mark, 0)
    for side in range(2):
        def number(i, count):
            here = place[side * blocks + i]
            lists_ref[side * room + count] = i
            place[side * blocks + i] = count
            return count + here

        lax.fori_loop(0, blocks, number, jnp.int32(0))

    def tell(pair, held):
        slot = group ^ first[best * pairs + pair]
        alive = slot < live[pair]
        now = (place[group * blocks + table[pair, slot, 0]], place[group * blocks + table[pair, slot, 1]], pair)
        held = tuple(jnp.where(alive, new, old) for new, old in zip(now, held))
        for k in range(3):
            meta_ref[k * pairs + pair] = held[k]
        meta_ref[3 * pairs + pair] = alive.astype(jnp.int32)
        return held

    lax.fori_loop(0, pairs, tell, (jnp.int32(0),) * 3)
    mine_ref[0] = group ^ first[best * pairs + lax.axis_index("kp")]


def plan(block_table, live_slots, blocks, caps, planes):
    pairs = live_slots.shape[0]
    first = choices_of(pairs)
    member = (first[None, :, :, None] ^ np.arange(2)) == np.arange(2)[:, None, None, None]
    member = member.reshape(2, CHOICES, 2 * pairs).astype(np.float32)
    room = caps[-1] + 8
    width = -(-(blocks + 1) // LANES) * LANES
    return pl.pallas_call(
        functools.partial(plan_kernel, pairs=pairs, blocks=blocks, caps=caps, room=room, planes=planes),
        in_specs=[SMEM, SMEM, SMEM, VMEM],
        out_specs=[SMEM, SMEM, SMEM, SMEM],
        out_shape=[jax.ShapeDtypeStruct((1,), jnp.int32), jax.ShapeDtypeStruct((1,), jnp.int32),
                   jax.ShapeDtypeStruct((2 * room,), jnp.int32), jax.ShapeDtypeStruct((4 * pairs,), jnp.int32)],
        scratch_shapes=[pltpu.VMEM((2 * pairs, width), jnp.float32), pltpu.SMEM((2 * blocks,), jnp.int32)],
    )(block_table, live_slots, jnp.asarray(first.reshape(-1)), jnp.asarray(member))


def gather_kernel(lists, store, *refs, cap, room, steps, planes, grains, begin, size):
    outs, sems = refs[:-1], refs[-1]
    me_plane = lax.axis_index("vr")
    copies = []
    for k, step in enumerate(steps):
        target = lax.rem(me_plane + step, planes)
        side, half = lax.rem(target, 2), lax.div(target, 2)
        for u in range(cap):
            block = lists[side * room + u]
            start = block * (grains * (planes // 2)) + half * grains + begin
            copy = pltpu.make_async_copy(store.at[pl.ds(start, size)], outs[k].at[u], sems.at[k, u])
            copy.start()
            copies.append(copy)
    for copy in copies:
        copy.wait()


def gather(lists, store, cap, room, steps, planes, grains, begin, size):
    grain, width = store.shape[1:]
    outs = pl.pallas_call(
        functools.partial(gather_kernel, cap=cap, room=room, steps=steps, planes=planes, grains=grains,
                          begin=begin, size=size),
        in_specs=[SMEM, ANY],
        out_specs=[VMEM] * len(steps),
        out_shape=[jax.ShapeDtypeStruct((cap, size, grain, width), store.dtype)] * len(steps),
        scratch_shapes=[pltpu.SemaphoreType.DMA((len(steps), cap))],
    )(lists, store)
    return [out.reshape(cap, size * grain, width) for out in outs]


def ladder_kernel(meta, *refs, pairs, rows, pitch, cols, planes, more):
    pieces, t_ref = refs[:planes], refs[planes]
    before = refs[planes + 1] if more else None
    out_ref, left, right, ts, order, sums = refs[planes + 1 + more:]
    item = pl.program_id(0)
    me_plane = lax.axis_index("vr")
    per = SLAB // planes
    half = cols // 2
    size = SLAB * pitch
    group = NO * NO * SLAB

    @pl.when(item == 0)
    def _():
        if rows < pitch:
            left[...] = jnp.zeros_like(left)
            right[...] = jnp.zeros_like(right)
        row = lax.broadcasted_iota(jnp.int32, (cols, cols), 0)
        col = lax.broadcasted_iota(jnp.int32, (cols, cols), 1)
        wanted = jnp.where(col < half, 2 * col, 2 * (col - half) + 1)
        order[...] = (row == wanted).astype(jnp.bfloat16)
        sums[...] = jnp.zeros_like(sums)

    @pl.when(meta[3 * pairs + item] > 0)
    def _():
        for step in range(planes):
            plane = lax.rem(me_plane + planes - step, planes)
            x = pieces[step][meta[item]].astype(jnp.float32)
            y = pieces[step][meta[pairs + item]].astype(jnp.float32)
            left[pl.ds(pl.multiple_of(plane * pitch, 8), rows), :] = x
            for sub in range(per):
                at = pl.ds(pl.multiple_of((plane * per + sub) * pitch, 8), rows)
                right[at, :] = y[:, sub * cols:(sub + 1) * cols]
        turned = [jnp.dot(left[:, sub * cols:(sub + 1) * cols].astype(jnp.bfloat16), order[...],
                          preferred_element_type=jnp.float32) for sub in range(per)]
        xs = jnp.concatenate([turned[sub][plane * pitch:(plane + 1) * pitch]
                              for plane in range(planes) for sub in range(per)], axis=0).astype(jnp.bfloat16)
        ys = right[...].astype(jnp.bfloat16)
        parts = []
        for n in range(NO * NO):
            ts[n, :half, :] = t_ref[0, n, :, :cols]
            ts[n, half:, :] = t_ref[0, n, :, cols:]
            z = jnp.dot(xs, ts[n], preferred_element_type=jnp.float32)
            high = z.astype(jnp.bfloat16)
            parts += [high, (z - high.astype(jnp.float32)).astype(jnp.bfloat16)]
        gram = lax.dot_general(jnp.concatenate(parts, axis=0), ys, (((1,), (1,)), ((), ())),
                               preferred_element_type=jnp.float32)
        row = lax.rem(lax.broadcasted_iota(jnp.int32, (size, size), 0), pitch)
        col = lax.rem(lax.broadcasted_iota(jnp.int32, (size, size), 1), pitch)
        for n in range(NO * NO):
            at = 2 * n * size
            term = jnp.where(row == col, gram[at:at + size] + gram[at + size:at + 2 * size], 0.0)
            sums[item, n * SLAB:(n + 1) * SLAB, :] = jnp.sum(term.reshape(SLAB, pitch, size), axis=1)

    @pl.when(item == pairs - 1)
    def _():
        pick = (lax.broadcasted_iota(jnp.int32, (size, SLAB), 0) // pitch
                == lax.broadcasted_iota(jnp.int32, (size, SLAB), 1)).astype(jnp.float32)
        total = jnp.dot(sums[...].reshape(pairs * group, size), pick, precision=lax.Precision.HIGHEST,
                        preferred_element_type=jnp.float32)
        out_ref[...] = total + before[...] if more else total


def ladder_part(meta, pieces, amps, cols, before):
    pairs = amps.shape[0]
    planes = len(pieces)
    rows, width = pieces[0].shape[1:]
    pitch = -(-rows // 8) * 8
    size = SLAB * pitch
    group = NO * NO * SLAB
    more = before is not None
    t_spec = pl.BlockSpec((1,) + amps.shape[1:], lambda i, m: (m[2 * pairs + i], 0, 0, 0))
    sum_spec = pl.BlockSpec((pairs * group, SLAB), lambda i, m: (0, 0))
    return pl.pallas_call(
        functools.partial(ladder_kernel, pairs=pairs, rows=rows, pitch=pitch, cols=cols, planes=planes, more=more),
        grid_spec=pltpu.PrefetchScalarGridSpec(
            num_scalar_prefetch=1,
            grid=(pairs,),
            in_specs=[VMEM] * planes + [t_spec] + [sum_spec] * more,
            out_specs=sum_spec,
            scratch_shapes=[
                pltpu.VMEM((planes * pitch, width), jnp.float32),
                pltpu.VMEM((size, cols), jnp.float32),
                pltpu.VMEM((NO * NO, cols, cols), jnp.bfloat16),
                pltpu.VMEM((cols, cols), jnp.bfloat16),
                pltpu.VMEM((pairs, group, size), jnp.float32),
            ],
        ),
        out_shape=jax.ShapeDtypeStruct((pairs * group, SLAB), jnp.float32),
        compiler_params=pltpu.CompilerParams(vmem_limit_bytes=ROOM),
        cost_estimate=pl.CostEstimate(
            flops=pairs * 2 * size * cols * (NO * NO * (cols + 2 * size) + cols),
            bytes_accessed=pairs * (NO * NO * cols * cols * 2 + 2 * planes * rows * width * 2),
            transcendentals=0),
    )(meta, *pieces, amps, *([before] if more else []))


def body(chol_store, amplitudes, block_table, live_slots, partner):
    ranks = lax.axis_size("kp")
    planes = lax.axis_size("vr")
    pairs, slots = block_table.shape[:2]
    blocks, depth, width = chol_store.shape
    cols = width * planes // SLAB
    per = SLAB // planes
    share = depth // (planes // slots)

    most = min(2 * pairs, blocks)
    caps = sorted({max(1, most * part // 16) for part in (9, 10, 11, 12, 16)})
    room = caps[-1] + 8
    branch, mine, lists, meta = plan(block_table, live_slots, blocks, caps, planes)

    amp = lax.dynamic_index_in_dim(amplitudes[0], mine[0], 0, keepdims=False)
    amp = amp.reshape(NO * NO, cols // 2, 2 * cols)

    grain = int(np.gcd(share, 8))
    grains = share // grain
    store = chol_store.reshape(blocks * depth // grain, grain, width)
    step_of = max(1, PITCH // grain)
    stages = [(g, min(step_of, grains - g)) for g in range(0, grains, step_of)]

    def run(cap, amp, lists, meta):
        amps = lax.all_gather(amp, "kp", axis=0, tiled=False)
        total = None
        others = tuple(sorted(range(1, planes), key=lambda step: -min(step, planes - step)))
        own = [gather(lists, store, cap, room, (0,), planes, grains, *stage)[0] for stage in stages]
        for k, stage in enumerate(stages):
            sent = []
            for steps in ((others[:1], others[1:]) if k == 0 else (others,)):
                sent += gather(lists, store, cap, room, steps, planes, grains, *stage)
            pieces = [own[k]] + [None] * (planes - 1)
            for step, piece in zip(others, sent):
                pieces[step] = lax.ppermute(piece, "vr", [(i, (i + step) % planes) for i in range(planes)])
            total = ladder_part(meta, pieces, amps, cols, total)
        return total

    total = lax.switch(branch[0], [functools.partial(run, cap) for cap in caps], amp, lists, meta)

    full = total.reshape(pairs, NO, NO, planes, per, SLAB).transpose(0, 3, 1, 2, 4, 5)
    other = total.reshape(pairs, NO, NO, SLAB, planes, per)[partner].transpose(0, 4, 2, 1, 5, 3)
    both = jnp.stack([full, other], axis=2).reshape(ranks * planes, 2 * NO * NO * per * SLAB)
    mine = lax.all_to_all(both, ("kp", "vr"), split_axis=0, concat_axis=0, tiled=True)
    mine = jnp.sum(mine, axis=0).reshape(2, 1, NO * NO, per, SLAB)
    return mine[0], mine[1]


def solution(mesh):
    placed = (P(None, "kp", "vr"), P("kp", None, None, None), P(), P(), P())
    return jax.shard_map(
        body,
        mesh=mesh,
        in_specs=placed,
        out_specs=(P("kp", None, "vr", None), P("kp", None, "vr", None)),
        check_vma=False,
    )
```

```python
import functools

import jax
import jax.numpy as jnp
import numpy as np
from jax import lax
from jax.experimental import pallas as pl
from jax.experimental.pallas import tpu as pltpu
from jax.sharding import PartitionSpec as P

NO = 2
SLAB = 8
PITCH = 32
LANES = 128
CHOICES = 128
ROOM = 58 * 2 ** 20
ANY = pl.BlockSpec(memory_space=pl.ANY)
SMEM = pl.BlockSpec(memory_space=pltpu.SMEM)
VMEM = pl.BlockSpec(memory_space=pltpu.VMEM)


def choices_of(pairs):
    if pairs <= 8:
        codes = np.arange(CHOICES)
        return ((codes[:, None] >> np.arange(pairs)) & 1).astype(np.int32)
    return np.random.RandomState(0).randint(0, 2, (CHOICES, pairs)).astype(np.int32)


def plan_kernel(table, live, first, member, branch_ref, mine_ref, lists_ref, meta_ref, touch, place,
                *, pairs, blocks, caps, room, planes):
    items = 2 * pairs
    group = lax.rem(lax.axis_index("vr"), 2)
    lane = lax.broadcasted_iota(jnp.int32, (1, touch.shape[1]), 1)
    for item in range(items):
        alive = (item % 2 < live[item // 2]).astype(jnp.int32)
        left = table[item // 2, item % 2, 0] * alive - (1 - alive)
        right = table[item // 2, item % 2, 1] * alive - (1 - alive)
        last = jnp.where(alive > 0, touch.shape[1] - 1, -1)
        touch[item:item + 1, :] = ((lane == left) | (lane == right) | (lane == last)).astype(jnp.float32)
    counts, loads = [], []
    for side in range(2):
        hits = jnp.dot(member[side], touch[...], preferred_element_type=jnp.float32)
        is_last = lane == touch.shape[1] - 1
        counts.append(jnp.sum(jnp.where(is_last, 0.0, (hits > 0.5).astype(jnp.float32)), axis=1, keepdims=True))
        loads.append(jnp.sum(jnp.where(is_last, hits, 0.0), axis=1, keepdims=True))
    need = jnp.maximum(counts[0], counts[1]) * (pairs + 1) + jnp.maximum(loads[0], loads[1])
    order = lax.broadcasted_iota(jnp.int32, need.shape, 0).astype(jnp.float32)
    code = jnp.min(need * CHOICES + order).astype(jnp.int32)
    best = lax.rem(code, CHOICES)
    need = lax.div(code, CHOICES * (pairs + 1))
    branch = jnp.int32(0)
    for cap in caps[:-1]:
        branch += (need > cap).astype(jnp.int32)
    branch_ref[0] = branch

    def clear(i, carry):
        place[i] = 0
        return carry

    lax.fori_loop(0, 2 * blocks, clear, 0)

    def empty(i, carry):
        lists_ref[i] = 0
        return carry

    lax.fori_loop(0, 2 * room, empty, 0)

    def mark(item, carry):
        pair = lax.div(item, 2)
        slot = lax.rem(item, 2)
        side = first[best * pairs + pair] ^ slot
        alive = (slot < live[pair]).astype(jnp.int32)
        for end in range(2):
            at = side * blocks + table[pair, slot, end]
            place[at] = place[at] | alive
        return carry

    lax.fori_loop(0, items, mark, 0)
    for side in range(2):
        def number(i, count):
            here = place[side * blocks + i]
            lists_ref[side * room + count] = i
            place[side * blocks + i] = count
            return count + here

        lax.fori_loop(0, blocks, number, jnp.int32(0))

    def tell(pair, count):
        slot = group ^ first[best * pairs + pair]
        meta_ref[count] = place[group * blocks + table[pair, slot, 0]]
        meta_ref[room + count] = place[group * blocks + table[pair, slot, 1]]
        meta_ref[2 * room + count] = pair
        return count + (slot < live[pair]).astype(jnp.int32)

    count = lax.fori_loop(0, pairs, tell, jnp.int32(0))
    meta_ref[3 * room] = count

    def fill(i, carry):
        for k in range(3):
            meta_ref[k * room + i] = meta_ref[k * room + jnp.maximum(count - 1, 0)]
        return carry

    lax.fori_loop(count, pairs, fill, 0)
    mine_ref[0] = group ^ first[best * pairs + lax.axis_index("kp")]


def plan(block_table, live_slots, blocks, caps, planes):
    pairs = live_slots.shape[0]
    first = choices_of(pairs)
    member = (first[None, :, :, None] ^ np.arange(2)) == np.arange(2)[:, None, None, None]
    member = member.reshape(2, CHOICES, 2 * pairs).astype(np.float32)
    room = caps[-1] + 8
    width = -(-(blocks + 1) // LANES) * LANES
    return pl.pallas_call(
        functools.partial(plan_kernel, pairs=pairs, blocks=blocks, caps=caps, room=room, planes=planes),
        in_specs=[SMEM, SMEM, SMEM, VMEM],
        out_specs=[SMEM, SMEM, SMEM, SMEM],
        out_shape=[jax.ShapeDtypeStruct((1,), jnp.int32), jax.ShapeDtypeStruct((1,), jnp.int32),
                   jax.ShapeDtypeStruct((2 * room,), jnp.int32), jax.ShapeDtypeStruct((3 * room + 1,), jnp.int32)],
        scratch_shapes=[pltpu.VMEM((2 * pairs, width), jnp.float32), pltpu.SMEM((2 * blocks,), jnp.int32)],
    )(block_table, live_slots, jnp.asarray(first.reshape(-1)), jnp.asarray(member))


def gather_kernel(lists, store, *refs, cap, room, steps, planes, grains, begin, size):
    outs, sems = refs[:-1], refs[-1]
    me_plane = lax.axis_index("vr")
    copies = []
    for k, step in enumerate(steps):
        target = lax.rem(me_plane + step, planes)
        side, half = lax.rem(target, 2), lax.div(target, 2)
        for u in range(cap):
            block = lists[side * room + u]
            start = block * (grains * (planes // 2)) + half * grains + begin
            copy = pltpu.make_async_copy(store.at[pl.ds(start, size)], outs[k].at[u], sems.at[k, u])
            copy.start()
            copies.append(copy)
    for copy in copies:
        copy.wait()


def gather(lists, store, cap, room, steps, planes, grains, begin, size):
    grain, width = store.shape[1:]
    outs = pl.pallas_call(
        functools.partial(gather_kernel, cap=cap, room=room, steps=steps, planes=planes, grains=grains,
                          begin=begin, size=size),
        in_specs=[SMEM, ANY],
        out_specs=[VMEM] * len(steps),
        out_shape=[jax.ShapeDtypeStruct((cap, size, grain, width), store.dtype)] * len(steps),
        scratch_shapes=[pltpu.SemaphoreType.DMA((len(steps), cap))],
    )(lists, store)
    return [out.reshape(cap, size * grain, width) for out in outs]


def ladder_kernel(meta, *refs, pairs, room, rows, pitch, cols, planes, more):
    pieces, t_ref = refs[:planes], refs[planes]
    before = refs[planes + 1] if more else None
    out_ref, left, right, ts, order, sums = refs[planes + 1 + more:]
    item = pl.program_id(0)
    me_plane = lax.axis_index("vr")
    per = SLAB // planes
    half = cols // 2
    size = SLAB * pitch
    group = NO * NO * SLAB

    @pl.when(item == 0)
    def _():
        if rows < pitch:
            left[...] = jnp.zeros_like(left)
            right[...] = jnp.zeros_like(right)
        row = lax.broadcasted_iota(jnp.int32, (cols, cols), 0)
        col = lax.broadcasted_iota(jnp.int32, (cols, cols), 1)
        wanted = jnp.where(col < half, 2 * col, 2 * (col - half) + 1)
        order[...] = (row == wanted).astype(jnp.bfloat16)
        sums[...] = jnp.zeros_like(sums)

    @pl.when(item < meta[3 * room])
    def _():
        for step in range(planes):
            plane = lax.rem(me_plane + planes - step, planes)
            x = pieces[step][meta[item]].astype(jnp.float32)
            y = pieces[step][meta[room + item]].astype(jnp.float32)
            left[pl.ds(pl.multiple_of(plane * pitch, 8), rows), :] = x
            for sub in range(per):
                at = pl.ds(pl.multiple_of((plane * per + sub) * pitch, 8), rows)
                right[at, :] = y[:, sub * cols:(sub + 1) * cols]
        turned = [jnp.dot(left[:, sub * cols:(sub + 1) * cols].astype(jnp.bfloat16), order[...],
                          preferred_element_type=jnp.float32) for sub in range(per)]
        xs = jnp.concatenate([turned[sub][plane * pitch:(plane + 1) * pitch]
                              for plane in range(planes) for sub in range(per)], axis=0).astype(jnp.bfloat16)
        ys = right[...].astype(jnp.bfloat16)
        parts = []
        for n in range(NO * NO):
            ts[n, :half, :] = t_ref[0, n, :, :cols]
            ts[n, half:, :] = t_ref[0, n, :, cols:]
            z = jnp.dot(xs, ts[n], preferred_element_type=jnp.float32)
            high = z.astype(jnp.bfloat16)
            parts += [high, (z - high.astype(jnp.float32)).astype(jnp.bfloat16)]
        gram = lax.dot_general(jnp.concatenate(parts, axis=0), ys, (((1,), (1,)), ((), ())),
                               preferred_element_type=jnp.float32)
        row = lax.rem(lax.broadcasted_iota(jnp.int32, (size, size), 0), pitch)
        col = lax.rem(lax.broadcasted_iota(jnp.int32, (size, size), 1), pitch)
        for n in range(NO * NO):
            at = 2 * n * size
            term = jnp.where(row == col, gram[at:at + size] + gram[at + size:at + 2 * size], 0.0)
            sums[meta[2 * room + item], n * SLAB:(n + 1) * SLAB, :] = jnp.sum(term.reshape(SLAB, pitch, size), axis=1)

    @pl.when(item == pairs - 1)
    def _():
        pick = (lax.broadcasted_iota(jnp.int32, (size, SLAB), 0) // pitch
                == lax.broadcasted_iota(jnp.int32, (size, SLAB), 1)).astype(jnp.float32)
        total = jnp.dot(sums[...].reshape(pairs * group, size), pick, precision=lax.Precision.HIGHEST,
                        preferred_element_type=jnp.float32)
        out_ref[...] = total + before[...] if more else total


def ladder_part(meta, pieces, amps, cols, room, before):
    pairs = amps.shape[0]
    planes = len(pieces)
    rows, width = pieces[0].shape[1:]
    pitch = -(-rows // 8) * 8
    size = SLAB * pitch
    group = NO * NO * SLAB
    more = before is not None
    t_spec = pl.BlockSpec((1,) + amps.shape[1:], lambda i, m: (m[2 * room + i], 0, 0, 0))
    sum_spec = VMEM
    return pl.pallas_call(
        functools.partial(ladder_kernel, pairs=pairs, room=room, rows=rows, pitch=pitch, cols=cols, planes=planes, more=more),
        grid_spec=pltpu.PrefetchScalarGridSpec(
            num_scalar_prefetch=1,
            grid=(pairs,),
            in_specs=[VMEM] * planes + [t_spec] + [sum_spec] * more,
            out_specs=sum_spec,
            scratch_shapes=[
                pltpu.VMEM((planes * pitch, width), jnp.float32),
                pltpu.VMEM((size, cols), jnp.float32),
                pltpu.VMEM((NO * NO, cols, cols), jnp.bfloat16),
                pltpu.VMEM((cols, cols), jnp.bfloat16),
                pltpu.VMEM((pairs, group, size), jnp.float32),
            ],
        ),
        out_shape=jax.ShapeDtypeStruct((pairs * group, SLAB), jnp.float32),
        compiler_params=pltpu.CompilerParams(vmem_limit_bytes=ROOM),
        cost_estimate=pl.CostEstimate(
            flops=pairs * 2 * size * cols * (NO * NO * (cols + 2 * size) + cols),
            bytes_accessed=pairs * (NO * NO * cols * cols * 2 + 2 * planes * rows * width * 2),
            transcendentals=0),
    )(meta, *pieces, amps, *([before] if more else []))


def body(chol_store, amplitudes, block_table, live_slots, partner):
    ranks = lax.axis_size("kp")
    planes = lax.axis_size("vr")
    pairs, slots = block_table.shape[:2]
    blocks, depth, width = chol_store.shape
    cols = width * planes // SLAB
    per = SLAB // planes
    share = depth // (planes // slots)

    most = min(2 * pairs, blocks)
    caps = sorted({max(1, most * part // 16) for part in (9, 10, 11, 12, 16)})
    room = caps[-1] + 8
    branch, mine, lists, meta = plan(block_table, live_slots, blocks, caps, planes)

    amp = lax.dynamic_index_in_dim(amplitudes[0], mine[0], 0, keepdims=False)
    amp = amp.reshape(NO * NO, cols // 2, 2 * cols)

    grain = int(np.gcd(share, 8))
    grains = share // grain
    store = chol_store.reshape(blocks * depth // grain, grain, width)
    step_of = max(1, PITCH // grain)
    stages = [(g, min(step_of, grains - g)) for g in range(0, grains, step_of)]

    def run(cap, amp, lists, meta):
        amps = lax.all_gather(amp, "kp", axis=0, tiled=False)
        total = None
        others = tuple(sorted(range(1, planes), key=lambda step: -min(step, planes - step)))
        own = [gather(lists, store, cap, room, (0,), planes, grains, *stage)[0] for stage in stages]
        for k, stage in enumerate(stages):
            sent = []
            for steps in ((others[:1], others[1:]) if k == 0 else (others,)):
                sent += gather(lists, store, cap, room, steps, planes, grains, *stage)
            pieces = [own[k]] + [None] * (planes - 1)
            for step, piece in zip(others, sent):
                pieces[step] = lax.ppermute(piece, "vr", [(i, (i + step) % planes) for i in range(planes)])
            total = ladder_part(meta, pieces, amps, cols, room, total)
        return total

    total = lax.switch(branch[0], [functools.partial(run, cap) for cap in caps], amp, lists, meta)

    full = total.reshape(pairs, NO, NO, planes, per, SLAB).transpose(0, 3, 1, 2, 4, 5)
    other = total.reshape(pairs, NO, NO, SLAB, planes, per)[partner].transpose(0, 4, 2, 1, 5, 3)
    both = jnp.stack([full, other], axis=2).reshape(ranks * planes, 2 * NO * NO * per * SLAB)
    mine = lax.all_to_all(both, ("kp", "vr"), split_axis=0, concat_axis=0, tiled=True)
    mine = jnp.sum(mine, axis=0).reshape(2, 1, NO * NO, per, SLAB)
    return mine[0], mine[1]


def solution(mesh):
    placed = (P(None, "kp", "vr"), P("kp", None, None, None), P(), P(), P())
    return jax.shard_map(
        body,
        mesh=mesh,
        in_specs=placed,
        out_specs=(P("kp", None, "vr", None), P("kp", None, "vr", None)),
        check_vma=False,
    )
```

```python
import functools

import jax
import jax.numpy as jnp
import numpy as np
from jax import lax
from jax.experimental import pallas as pl
from jax.experimental.pallas import tpu as pltpu
from jax.sharding import PartitionSpec as P

NO = 2
SLAB = 8
PITCH = 32
LANES = 128
CHOICES = 128
ROOM = 58 * 2 ** 20
ANY = pl.BlockSpec(memory_space=pl.ANY)
SMEM = pl.BlockSpec(memory_space=pltpu.SMEM)
VMEM = pl.BlockSpec(memory_space=pltpu.VMEM)


def choices_of(pairs):
    if pairs <= 8:
        codes = np.arange(CHOICES)
        return ((codes[:, None] >> np.arange(pairs)) & 1).astype(np.int32)
    return np.random.RandomState(0).randint(0, 2, (CHOICES, pairs)).astype(np.int32)


def repeat(times, step, carry):
    def eight(k, carry):
        for j in range(8):
            carry = step(8 * k + j, carry)
        return carry

    whole = times // 8
    carry = lax.fori_loop(0, whole, eight, carry)
    for i in range(8 * whole, times):
        carry = step(i, carry)
    return carry


def plan_kernel(table, live, first, member, branch_ref, mine_ref, lists_ref, meta_ref, touch, place,
                *, pairs, blocks, caps, room, planes):
    items = 2 * pairs
    group = lax.rem(lax.axis_index("vr"), 2)
    lane = lax.broadcasted_iota(jnp.int32, (1, touch.shape[1]), 1)
    for item in range(items):
        alive = (item % 2 < live[item // 2]).astype(jnp.int32)
        left = table[item % 2, 0, item // 2] * alive - (1 - alive)
        right = table[item % 2, 1, item // 2] * alive - (1 - alive)
        last = jnp.where(alive > 0, touch.shape[1] - 1, -1)
        touch[item:item + 1, :] = ((lane == left) | (lane == right) | (lane == last)).astype(jnp.float32)
    counts, loads = [], []
    for side in range(2):
        hits = jnp.dot(member[side], touch[...], preferred_element_type=jnp.float32)
        is_last = lane == touch.shape[1] - 1
        counts.append(jnp.sum(jnp.where(is_last, 0.0, (hits > 0.5).astype(jnp.float32)), axis=1, keepdims=True))
        loads.append(jnp.sum(jnp.where(is_last, hits, 0.0), axis=1, keepdims=True))
    need = jnp.maximum(counts[0], counts[1]) * (pairs + 1) + jnp.maximum(loads[0], loads[1])
    order = lax.broadcasted_iota(jnp.int32, need.shape, 0).astype(jnp.float32)
    code = jnp.min(need * CHOICES + order).astype(jnp.int32)
    best = lax.rem(code, CHOICES)
    need = lax.div(code, CHOICES * (pairs + 1))
    branch = jnp.int32(0)
    for cap in caps[:-1]:
        branch += (need > cap).astype(jnp.int32)
    branch_ref[0] = branch

    def clear(i, carry):
        place[i] = 0
        return carry

    repeat(2 * blocks, clear, 0)

    def empty(i, carry):
        lists_ref[i] = 0
        return carry

    repeat(2 * room, empty, 0)

    def mark(item, carry):
        pair = lax.div(item, 2)
        slot = lax.rem(item, 2)
        side = first[best * pairs + pair] ^ slot
        alive = (slot < live[pair]).astype(jnp.int32)
        for end in range(2):
            at = side * blocks + table[slot, end, pair]
            place[at] = place[at] | alive
        return carry

    repeat(items, mark, 0)
    for side in range(2):
        def number(i, count):
            here = place[side * blocks + i]
            lists_ref[side * room + count] = i
            place[side * blocks + i] = count
            return count + here

        repeat(blocks, number, jnp.int32(0))

    def tell(pair, count):
        slot = group ^ first[best * pairs + pair]
        meta_ref[count] = place[group * blocks + table[slot, 0, pair]]
        meta_ref[room + count] = place[group * blocks + table[slot, 1, pair]]
        meta_ref[2 * room + count] = pair
        return count + (slot < live[pair]).astype(jnp.int32)

    count = repeat(pairs, tell, jnp.int32(0))
    meta_ref[3 * room] = count

    def fill(i, carry):
        for k in range(3):
            meta_ref[k * room + i] = meta_ref[k * room + jnp.maximum(count - 1, 0)]
        return carry

    lax.fori_loop(count, pairs, fill, 0)
    mine_ref[0] = group ^ first[best * pairs + lax.axis_index("kp")]


def plan(block_table, live_slots, blocks, caps, planes):
    pairs = live_slots.shape[0]
    first = choices_of(pairs)
    member = (first[None, :, :, None] ^ np.arange(2)) == np.arange(2)[:, None, None, None]
    member = member.reshape(2, CHOICES, 2 * pairs).astype(np.float32)
    room = caps[-1] + 8
    width = -(-(blocks + 1) // LANES) * LANES
    return pl.pallas_call(
        functools.partial(plan_kernel, pairs=pairs, blocks=blocks, caps=caps, room=room, planes=planes),
        in_specs=[SMEM, SMEM, SMEM, VMEM],
        out_specs=[SMEM, SMEM, SMEM, SMEM],
        out_shape=[jax.ShapeDtypeStruct((1,), jnp.int32), jax.ShapeDtypeStruct((1,), jnp.int32),
                   jax.ShapeDtypeStruct((2 * room,), jnp.int32), jax.ShapeDtypeStruct((3 * room + 1,), jnp.int32)],
        scratch_shapes=[pltpu.VMEM((2 * pairs, width), jnp.float32), pltpu.SMEM((2 * blocks,), jnp.int32)],
    )(block_table.transpose(1, 2, 0), live_slots, jnp.asarray(first.reshape(-1)), jnp.asarray(member))


def gather_kernel(lists, store, *refs, cap, room, steps, planes, grains, begin, size):
    outs, sems = refs[:-1], refs[-1]
    me_plane = lax.axis_index("vr")
    copies = []
    for k, step in enumerate(steps):
        target = lax.rem(me_plane + step, planes)
        side, half = lax.rem(target, 2), lax.div(target, 2)
        for u in range(cap):
            block = lists[side * room + u]
            start = block * (grains * (planes // 2)) + half * grains + begin
            copy = pltpu.make_async_copy(store.at[pl.ds(start, size)], outs[k].at[u], sems.at[k, u])
            copy.start()
            copies.append(copy)
    for copy in copies:
        copy.wait()


def gather(lists, store, cap, room, steps, planes, grains, begin, size):
    grain, width = store.shape[1:]
    outs = pl.pallas_call(
        functools.partial(gather_kernel, cap=cap, room=room, steps=steps, planes=planes, grains=grains,
                          begin=begin, size=size),
        in_specs=[SMEM, ANY],
        out_specs=[VMEM] * len(steps),
        out_shape=[jax.ShapeDtypeStruct((cap, size, grain, width), store.dtype)] * len(steps),
        scratch_shapes=[pltpu.SemaphoreType.DMA((len(steps), cap))],
    )(lists, store)
    return [out.reshape(cap, size * grain, width) for out in outs]


def ladder_kernel(meta, *refs, pairs, room, rows, pitch, cols, planes, more):
    pieces, t_ref = refs[:planes], refs[planes]
    before = refs[planes + 1] if more else None
    out_ref, left, right, ts, order, sums = refs[planes + 1 + more:]
    item = pl.program_id(0)
    me_plane = lax.axis_index("vr")
    per = SLAB // planes
    half = cols // 2
    size = SLAB * pitch
    group = NO * NO * SLAB

    @pl.when(item == 0)
    def _():
        if rows < pitch:
            left[...] = jnp.zeros_like(left)
            right[...] = jnp.zeros_like(right)
        row = lax.broadcasted_iota(jnp.int32, (cols, cols), 0)
        col = lax.broadcasted_iota(jnp.int32, (cols, cols), 1)
        wanted = jnp.where(col < half, 2 * col, 2 * (col - half) + 1)
        order[...] = (row == wanted).astype(jnp.bfloat16)
        sums[...] = jnp.zeros_like(sums)

    @pl.when(item < meta[3 * room])
    def _():
        for step in range(planes):
            plane = lax.rem(me_plane + planes - step, planes)
            x = pieces[step][meta[item]].astype(jnp.float32)
            y = pieces[step][meta[room + item]].astype(jnp.float32)
            left[pl.ds(pl.multiple_of(plane * pitch, 8), rows), :] = x
            for sub in range(per):
                at = pl.ds(pl.multiple_of((plane * per + sub) * pitch, 8), rows)
                right[at, :] = y[:, sub * cols:(sub + 1) * cols]
        turned = [jnp.dot(left[:, sub * cols:(sub + 1) * cols].astype(jnp.bfloat16), order[...],
                          preferred_element_type=jnp.float32) for sub in range(per)]
        xs = jnp.concatenate([turned[sub][plane * pitch:(plane + 1) * pitch]
                              for plane in range(planes) for sub in range(per)], axis=0).astype(jnp.bfloat16)
        ys = right[...].astype(jnp.bfloat16)
        parts = []
        for n in range(NO * NO):
            ts[n, :half, :] = t_ref[0, n, :, :cols]
            ts[n, half:, :] = t_ref[0, n, :, cols:]
            z = jnp.dot(xs, ts[n], preferred_element_type=jnp.float32)
            high = z.astype(jnp.bfloat16)
            parts += [high, (z - high.astype(jnp.float32)).astype(jnp.bfloat16)]
        gram = lax.dot_general(jnp.concatenate(parts, axis=0), ys, (((1,), (1,)), ((), ())),
                               preferred_element_type=jnp.float32)
        row = lax.rem(lax.broadcasted_iota(jnp.int32, (size, size), 0), pitch)
        col = lax.rem(lax.broadcasted_iota(jnp.int32, (size, size), 1), pitch)
        for n in range(NO * NO):
            at = 2 * n * size
            term = jnp.where(row == col, gram[at:at + size] + gram[at + size:at + 2 * size], 0.0)
            sums[meta[2 * room + item], n * SLAB:(n + 1) * SLAB, :] = jnp.sum(term.reshape(SLAB, pitch, size), axis=1)

    @pl.when(item == pairs - 1)
    def _():
        pick = (lax.broadcasted_iota(jnp.int32, (size, SLAB), 0) // pitch
                == lax.broadcasted_iota(jnp.int32, (size, SLAB), 1)).astype(jnp.float32)
        total = jnp.dot(sums[...].reshape(pairs * group, size), pick, precision=lax.Precision.HIGHEST,
                        preferred_element_type=jnp.float32)
        out_ref[...] = total + before[...] if more else total


def ladder_part(meta, pieces, amps, cols, room, before):
    pairs = amps.shape[0]
    planes = len(pieces)
    rows, width = pieces[0].shape[1:]
    pitch = -(-rows // 8) * 8
    size = SLAB * pitch
    group = NO * NO * SLAB
    more = before is not None
    t_spec = pl.BlockSpec((1,) + amps.shape[1:], lambda i, m: (m[2 * room + i], 0, 0, 0))
    sum_spec = VMEM
    return pl.pallas_call(
        functools.partial(ladder_kernel, pairs=pairs, room=room, rows=rows, pitch=pitch, cols=cols, planes=planes, more=more),
        grid_spec=pltpu.PrefetchScalarGridSpec(
            num_scalar_prefetch=1,
            grid=(pairs,),
            in_specs=[VMEM] * planes + [t_spec] + [sum_spec] * more,
            out_specs=sum_spec,
            scratch_shapes=[
                pltpu.VMEM((planes * pitch, width), jnp.float32),
                pltpu.VMEM((size, cols), jnp.float32),
                pltpu.VMEM((NO * NO, cols, cols), jnp.bfloat16),
                pltpu.VMEM((cols, cols), jnp.bfloat16),
                pltpu.VMEM((pairs, group, size), jnp.float32),
            ],
        ),
        out_shape=jax.ShapeDtypeStruct((pairs * group, SLAB), jnp.float32),
        compiler_params=pltpu.CompilerParams(vmem_limit_bytes=ROOM),
        cost_estimate=pl.CostEstimate(
            flops=pairs * 2 * size * cols * (NO * NO * (cols + 2 * size) + cols),
            bytes_accessed=pairs * (NO * NO * cols * cols * 2 + 2 * planes * rows * width * 2),
            transcendentals=0),
    )(meta, *pieces, amps, *([before] if more else []))


def body(chol_store, amplitudes, block_table, live_slots, partner):
    ranks = lax.axis_size("kp")
    planes = lax.axis_size("vr")
    pairs, slots = block_table.shape[:2]
    blocks, depth, width = chol_store.shape
    cols = width * planes // SLAB
    per = SLAB // planes
    share = depth // (planes // slots)

    most = min(2 * pairs, blocks)
    caps = sorted({max(1, most * part // 16) for part in (9, 10, 11, 12, 16)})
    room = caps[-1] + 8
    branch, mine, lists, meta = plan(block_table, live_slots, blocks, caps, planes)

    amp = lax.dynamic_index_in_dim(amplitudes[0], mine[0], 0, keepdims=False)
    amp = amp.reshape(NO * NO, cols // 2, 2 * cols)

    grain = int(np.gcd(share, 8))
    grains = share // grain
    store = chol_store.reshape(blocks * depth // grain, grain, width)
    step_of = max(1, PITCH // grain)
    stages = [(g, min(step_of, grains - g)) for g in range(0, grains, step_of)]

    def run(cap, amp, lists, meta):
        amps = lax.all_gather(amp, "kp", axis=0, tiled=False)
        total = None
        others = tuple(sorted(range(1, planes), key=lambda step: -min(step, planes - step)))
        own = [gather(lists, store, cap, room, (0,), planes, grains, *stage)[0] for stage in stages]
        for k, stage in enumerate(stages):
            sent = []
            for steps in ((others[:1], others[1:]) if k == 0 else (others,)):
                sent += gather(lists, store, cap, room, steps, planes, grains, *stage)
            pieces = [own[k]] + [None] * (planes - 1)
            for step, piece in zip(others, sent):
                pieces[step] = lax.ppermute(piece, "vr", [(i, (i + step) % planes) for i in range(planes)])
            total = ladder_part(meta, pieces, amps, cols, room, total)
        return total

    total = lax.switch(branch[0], [functools.partial(run, cap) for cap in caps], amp, lists, meta)

    full = total.reshape(pairs, NO, NO, planes, per, SLAB).transpose(0, 3, 1, 2, 4, 5)
    other = total.reshape(pairs, NO, NO, SLAB, planes, per)[partner].transpose(0, 4, 2, 1, 5, 3)
    both = jnp.stack([full, other], axis=2).reshape(ranks * planes, 2 * NO * NO * per * SLAB)
    mine = lax.all_to_all(both, ("kp", "vr"), split_axis=0, concat_axis=0, tiled=True)
    mine = jnp.sum(mine, axis=0).reshape(2, 1, NO * NO, per, SLAB)
    return mine[0], mine[1]


def solution(mesh):
    placed = (P(None, "kp", "vr"), P("kp", None, None, None), P(), P(), P())
    return jax.shard_map(
        body,
        mesh=mesh,
        in_specs=placed,
        out_specs=(P("kp", None, "vr", None), P("kp", None, "vr", None)),
        check_vma=False,
    )
```

```python
import functools

import jax
import jax.numpy as jnp
import numpy as np
from jax import lax
from jax.experimental import pallas as pl
from jax.experimental.pallas import tpu as pltpu
from jax.sharding import PartitionSpec as P

NO = 2
SLAB = 8
PITCH = 32
LANES = 128
CHOICES = 128
ROOM = 32 * 2 ** 20
ANY = pl.BlockSpec(memory_space=pl.ANY)
SMEM = pl.BlockSpec(memory_space=pltpu.SMEM)
VMEM = pl.BlockSpec(memory_space=pltpu.VMEM)


def choices_of(pairs):
    if pairs <= 8:
        codes = np.arange(CHOICES)
        return ((codes[:, None] >> np.arange(pairs)) & 1).astype(np.int32)
    return np.random.RandomState(0).randint(0, 2, (CHOICES, pairs)).astype(np.int32)


def repeat(times, step, carry):
    def eight(k, carry):
        for j in range(8):
            carry = step(8 * k + j, carry)
        return carry

    whole = times // 8
    carry = lax.fori_loop(0, whole, eight, carry)
    for i in range(8 * whole, times):
        carry = step(i, carry)
    return carry


def plan_kernel(table, live, first, member, branch_ref, mine_ref, lists_ref, meta_ref, touch, place,
                *, pairs, blocks, caps, room, planes):
    items = 2 * pairs
    group = lax.rem(lax.axis_index("vr"), 2)
    lane = lax.broadcasted_iota(jnp.int32, (1, touch.shape[1]), 1)
    for item in range(items):
        alive = (item % 2 < live[item // 2]).astype(jnp.int32)
        left = table[item % 2, 0, item // 2] * alive - (1 - alive)
        right = table[item % 2, 1, item // 2] * alive - (1 - alive)
        last = jnp.where(alive > 0, touch.shape[1] - 1, -1)
        touch[item:item + 1, :] = ((lane == left) | (lane == right) | (lane == last)).astype(jnp.float32)
    counts, loads = [], []
    for side in range(2):
        hits = jnp.dot(member[side], touch[...], preferred_element_type=jnp.float32)
        is_last = lane == touch.shape[1] - 1
        counts.append(jnp.sum(jnp.where(is_last, 0.0, (hits > 0.5).astype(jnp.float32)), axis=1, keepdims=True))
        loads.append(jnp.sum(jnp.where(is_last, hits, 0.0), axis=1, keepdims=True))
    need = jnp.maximum(counts[0], counts[1]) * (pairs + 1) + jnp.maximum(loads[0], loads[1])
    order = lax.broadcasted_iota(jnp.int32, need.shape, 0).astype(jnp.float32)
    code = jnp.min(need * CHOICES + order).astype(jnp.int32)
    best = lax.rem(code, CHOICES)
    need = lax.div(code, CHOICES * (pairs + 1))
    branch = jnp.int32(0)
    for cap in caps[:-1]:
        branch += (need > cap).astype(jnp.int32)
    branch_ref[0] = branch

    def clear(i, carry):
        place[i] = 0
        return carry

    repeat(2 * blocks, clear, 0)

    def empty(i, carry):
        lists_ref[i] = 0
        return carry

    repeat(2 * room, empty, 0)

    def mark(item, carry):
        pair = lax.div(item, 2)
        slot = lax.rem(item, 2)
        side = first[best * pairs + pair] ^ slot
        alive = (slot < live[pair]).astype(jnp.int32)
        for end in range(2):
            at = side * blocks + table[slot, end, pair]
            place[at] = place[at] | alive
        return carry

    repeat(items, mark, 0)
    for side in range(2):
        def number(i, count):
            here = place[side * blocks + i]
            lists_ref[side * room + count] = i
            place[side * blocks + i] = count
            return count + here

        repeat(blocks, number, jnp.int32(0))

    def tell(pair, count):
        slot = group ^ first[best * pairs + pair]
        meta_ref[count] = place[group * blocks + table[slot, 0, pair]]
        meta_ref[room + count] = place[group * blocks + table[slot, 1, pair]]
        meta_ref[2 * room + count] = pair
        return count + (slot < live[pair]).astype(jnp.int32)

    count = repeat(pairs, tell, jnp.int32(0))
    meta_ref[3 * room] = count

    def fill(i, carry):
        for k in range(3):
            meta_ref[k * room + i] = meta_ref[k * room + jnp.maximum(count - 1, 0)]
        return carry

    lax.fori_loop(count, pairs, fill, 0)
    mine_ref[0] = group ^ first[best * pairs + lax.axis_index("kp")]


def plan(block_table, live_slots, blocks, caps, planes):
    pairs = live_slots.shape[0]
    first = choices_of(pairs)
    member = (first[None, :, :, None] ^ np.arange(2)) == np.arange(2)[:, None, None, None]
    member = member.reshape(2, CHOICES, 2 * pairs).astype(np.float32)
    room = caps[-1] + 8
    width = -(-(blocks + 1) // LANES) * LANES
    return pl.pallas_call(
        functools.partial(plan_kernel, pairs=pairs, blocks=blocks, caps=caps, room=room, planes=planes),
        in_specs=[SMEM, SMEM, SMEM, VMEM],
        out_specs=[SMEM, SMEM, SMEM, SMEM],
        out_shape=[jax.ShapeDtypeStruct((1,), jnp.int32), jax.ShapeDtypeStruct((1,), jnp.int32),
                   jax.ShapeDtypeStruct((2 * room,), jnp.int32), jax.ShapeDtypeStruct((3 * room + 1,), jnp.int32)],
        scratch_shapes=[pltpu.VMEM((2 * pairs, width), jnp.float32), pltpu.SMEM((2 * blocks,), jnp.int32)],
    )(block_table.transpose(1, 2, 0), live_slots, jnp.asarray(first.reshape(-1)), jnp.asarray(member))


def gather_kernel(lists, store, *refs, cap, room, steps, planes, grains, begin, size):
    outs, sems = refs[:-1], refs[-1]
    me_plane = lax.axis_index("vr")
    copies = []
    for k, step in enumerate(steps):
        target = lax.rem(me_plane + step, planes)
        side, half = lax.rem(target, 2), lax.div(target, 2)
        for u in range(cap):
            block = lists[side * room + u]
            start = block * (grains * (planes // 2)) + half * grains + begin
            copy = pltpu.make_async_copy(store.at[pl.ds(start, size)], outs[k].at[u], sems.at[k, u])
            copy.start()
            copies.append(copy)
    for copy in copies:
        copy.wait()


def gather(lists, store, cap, room, steps, planes, grains, begin, size):
    grain, width = store.shape[1:]
    outs = pl.pallas_call(
        functools.partial(gather_kernel, cap=cap, room=room, steps=steps, planes=planes, grains=grains,
                          begin=begin, size=size),
        in_specs=[SMEM, ANY],
        out_specs=[VMEM] * len(steps),
        out_shape=[jax.ShapeDtypeStruct((cap, size, grain, width), store.dtype)] * len(steps),
        scratch_shapes=[pltpu.SemaphoreType.DMA((len(steps), cap))],
    )(lists, store)
    return [out.reshape(cap, size * grain, width) for out in outs]


def ladder_kernel(meta, *refs, pairs, room, rows, pitch, cols, planes, more):
    pieces, t_ref = refs[:planes], refs[planes]
    before = refs[planes + 1] if more else None
    out_ref, left, right, ts, order, sums = refs[planes + 1 + more:]
    item = pl.program_id(0)
    me_plane = lax.axis_index("vr")
    per = SLAB // planes
    half = cols // 2
    size = SLAB * pitch
    group = NO * NO * SLAB

    @pl.when(item == 0)
    def _():
        if rows < pitch:
            left[...] = jnp.zeros_like(left)
            right[...] = jnp.zeros_like(right)
        row = lax.broadcasted_iota(jnp.int32, (cols, cols), 0)
        col = lax.broadcasted_iota(jnp.int32, (cols, cols), 1)
        wanted = jnp.where(col < half, 2 * col, 2 * (col - half) + 1)
        order[...] = (row == wanted).astype(jnp.bfloat16)
        sums[...] = jnp.zeros_like(sums)

    @pl.when(item < meta[3 * room])
    def _():
        for step in range(planes):
            plane = lax.rem(me_plane + planes - step, planes)
            x = pieces[step][meta[item]].astype(jnp.float32)
            y = pieces[step][meta[room + item]].astype(jnp.float32)
            left[pl.ds(pl.multiple_of(plane * pitch, 8), rows), :] = x
            for sub in range(per):
                at = pl.ds(pl.multiple_of((plane * per + sub) * pitch, 8), rows)
                right[at, :] = y[:, sub * cols:(sub + 1) * cols]
        turned = [jnp.dot(left[:, sub * cols:(sub + 1) * cols].astype(jnp.bfloat16), order[...],
                          preferred_element_type=jnp.float32) for sub in range(per)]
        xs = jnp.concatenate([turned[sub][plane * pitch:(plane + 1) * pitch]
                              for plane in range(planes) for sub in range(per)], axis=0).astype(jnp.bfloat16)
        ys = right[...].astype(jnp.bfloat16)
        parts = []
        for n in range(NO * NO):
            ts[n, :half, :] = t_ref[0, n, :, :cols]
            ts[n, half:, :] = t_ref[0, n, :, cols:]
            z = jnp.dot(xs, ts[n], preferred_element_type=jnp.float32)
            high = z.astype(jnp.bfloat16)
            parts += [high, (z - high.astype(jnp.float32)).astype(jnp.bfloat16)]
        gram = lax.dot_general(jnp.concatenate(parts, axis=0), ys, (((1,), (1,)), ((), ())),
                               preferred_element_type=jnp.float32)
        row = lax.rem(lax.broadcasted_iota(jnp.int32, (size, size), 0), pitch)
        col = lax.rem(lax.broadcasted_iota(jnp.int32, (size, size), 1), pitch)
        for n in range(NO * NO):
            at = 2 * n * size
            term = jnp.where(row == col, gram[at:at + size] + gram[at + size:at + 2 * size], 0.0)
            sums[meta[2 * room + item], n * SLAB:(n + 1) * SLAB, :] = jnp.sum(term.reshape(SLAB, pitch, size), axis=1)

    @pl.when(item == pairs - 1)
    def _():
        pick = (lax.broadcasted_iota(jnp.int32, (size, SLAB), 0) // pitch
                == lax.broadcasted_iota(jnp.int32, (size, SLAB), 1)).astype(jnp.float32)
        total = jnp.dot(sums[...].reshape(pairs * group, size), pick, precision=lax.Precision.HIGHEST,
                        preferred_element_type=jnp.float32)
        out_ref[...] = total + before[...] if more else total


def ladder_part(meta, pieces, amps, cols, room, before):
    pairs = amps.shape[0]
    planes = len(pieces)
    rows, width = pieces[0].shape[1:]
    pitch = -(-rows // 8) * 8
    size = SLAB * pitch
    group = NO * NO * SLAB
    more = before is not None
    t_spec = pl.BlockSpec((1,) + amps.shape[1:], lambda i, m: (m[2 * room + i], 0, 0, 0))
    sum_spec = VMEM
    return pl.pallas_call(
        functools.partial(ladder_kernel, pairs=pairs, room=room, rows=rows, pitch=pitch, cols=cols, planes=planes, more=more),
        grid_spec=pltpu.PrefetchScalarGridSpec(
            num_scalar_prefetch=1,
            grid=(pairs,),
            in_specs=[VMEM] * planes + [t_spec] + [sum_spec] * more,
            out_specs=sum_spec,
            scratch_shapes=[
                pltpu.VMEM((planes * pitch, width), jnp.float32),
                pltpu.VMEM((size, cols), jnp.float32),
                pltpu.VMEM((NO * NO, cols, cols), jnp.bfloat16),
                pltpu.VMEM((cols, cols), jnp.bfloat16),
                pltpu.VMEM((pairs, group, size), jnp.float32),
            ],
        ),
        out_shape=jax.ShapeDtypeStruct((pairs * group, SLAB), jnp.float32),
        compiler_params=pltpu.CompilerParams(vmem_limit_bytes=ROOM),
        cost_estimate=pl.CostEstimate(
            flops=pairs * 2 * size * cols * (NO * NO * (cols + 2 * size) + cols),
            bytes_accessed=pairs * (NO * NO * cols * cols * 2 + 2 * planes * rows * width * 2),
            transcendentals=0),
    )(meta, *pieces, amps, *([before] if more else []))


def body(chol_store, amplitudes, block_table, live_slots, partner):
    ranks = lax.axis_size("kp")
    planes = lax.axis_size("vr")
    pairs, slots = block_table.shape[:2]
    blocks, depth, width = chol_store.shape
    cols = width * planes // SLAB
    per = SLAB // planes
    share = depth // (planes // slots)

    most = min(2 * pairs, blocks)
    caps = sorted({max(1, most * part // 16) for part in (9, 10, 11, 12, 16)})
    room = caps[-1] + 8
    branch, mine, lists, meta = plan(block_table, live_slots, blocks, caps, planes)

    amp = lax.dynamic_index_in_dim(amplitudes[0], mine[0], 0, keepdims=False)
    amp = amp.reshape(NO * NO, cols // 2, 2 * cols)

    grain = int(np.gcd(share, 8))
    grains = share // grain
    store = chol_store.reshape(blocks * depth // grain, grain, width)
    step_of = max(1, PITCH // grain)
    stages = [(g, min(step_of, grains - g)) for g in range(0, grains, step_of)]

    def run(cap, amp, lists, meta):
        amps = lax.all_gather(amp, "kp", axis=0, tiled=False)
        total = None
        others = tuple(sorted(range(1, planes), key=lambda step: -min(step, planes - step)))
        own = [gather(lists, store, cap, room, (0,), planes, grains, *stage)[0] for stage in stages]
        for k, stage in enumerate(stages):
            sent = []
            for steps in ((others[:1], others[1:]) if k == 0 else (others,)):
                sent += gather(lists, store, cap, room, steps, planes, grains, *stage)
            pieces = [own[k]] + [None] * (planes - 1)
            for step, piece in zip(others, sent):
                pieces[step] = lax.ppermute(piece, "vr", [(i, (i + step) % planes) for i in range(planes)])
            total = ladder_part(meta, pieces, amps, cols, room, total)
        return total

    total = lax.switch(branch[0], [functools.partial(run, cap) for cap in caps], amp, lists, meta)

    full = total.reshape(pairs, NO, NO, planes, per, SLAB).transpose(0, 3, 1, 2, 4, 5)
    other = total.reshape(pairs, NO, NO, SLAB, planes, per)[partner].transpose(0, 4, 2, 1, 5, 3)
    both = jnp.stack([full, other], axis=2).reshape(ranks * planes, 2 * NO * NO * per * SLAB)
    mine = lax.all_to_all(both, ("kp", "vr"), split_axis=0, concat_axis=0, tiled=True)
    mine = jnp.sum(mine, axis=0).reshape(2, 1, NO * NO, per, SLAB)
    return mine[0], mine[1]


def solution(mesh):
    placed = (P(None, "kp", "vr"), P("kp", None, None, None), P(), P(), P())
    return jax.shard_map(
        body,
        mesh=mesh,
        in_specs=placed,
        out_specs=(P("kp", None, "vr", None), P("kp", None, "vr", None)),
        check_vma=False,
    )
```
